256 devices in a mesh: tm: 8 (over x, core), rows: 32 (over z, y).
Axes of the slice: x: 4, y: 4, z: 8, core: 2. Of those that a mesh axis runs over, the one named last changes fastest.
Arguments:
- features: bfloat16 [16, 192, 32, 384], P('tm', 'rows'), may hold values from -6 to 6
- norm_gain: float32 [384], replicated, may hold values from 0.1 to 1.9
- res_weight: bfloat16 [3, 3, 3, 384, 384], replicated, may hold values from -0.0625 to 0.0625
- time_weight: bfloat16 [3, 384, 768], replicated, may hold values from -0.1875 to 0.1875
- up_weight: bfloat16 [3, 3, 384, 192], replicated, may hold values from -0.109375 to 0.109375
Outputs:
- decoded: bfloat16 [32, 384, 64, 192], P('tm', 'rows')
The draws below stay inside these ranges and needn't reach their ends.
All inputs are finite; a program needn't handle non-finite values.
Results may differ from the reference program's by a relative error of at most 0.0059.
Values may be sent and summed in bfloat16 or wider, within the bound.
No kernel may reach another device: no remote copies, remote signals or barrier semaphores. Data moves between devices by JAX's collectives and lax.ppermute only.
A program may use at most 128 MiB of HBM per device.

```python
import jax
import jax.numpy as jnp
from jax import lax

C = 384
CO = 192
COLUMNS = 32
FRAMES = 16
HEIGHT = 192


def levels(rng, extent, pieces, least, largest):
    factor_of = 1.0
    for position, shards_of in pieces:
        heights = jax.random.uniform(jax.random.fold_in(jax.random.fold_in(rng, 6), position), (shards_of,), jnp.float32, least / len(pieces), largest / len(pieces))
        factor_of = factor_of * jnp.repeat(jnp.exp(heights), extent[position] // shards_of).reshape((-1,) + (1,) * (len(extent) - 1 - position))
    return factor_of


def centred(stream_key, extent, scale, limit, shards=(), held_as=jnp.bfloat16):
    level = levels(stream_key, extent, shards, -0.22, 0.18) if shards else 1.0
    values = jax.random.normal(stream_key, extent, jnp.float32) * scale * level
    return jnp.minimum(jnp.maximum(values, -limit), limit).astype(held_as)


def setup_inputs(seed: int = 0) -> dict:
    seeds = jax.random.split(jax.random.key(seed), 6)
    return {
        "features": centred(seeds[0], (FRAMES, HEIGHT, COLUMNS, C), 1.0, 6.0, ((0, 8), (1, 32))),
        "norm_gain": jnp.clip(1.0 + 0.18 * jax.random.normal(seeds[1], (C,), jnp.float32), 0.1, 1.9),
        "res_weight": centred(seeds[2], (3, 3, 3, C, C), (27 * C) ** -0.5, 0.0625),
        "time_weight": centred(seeds[3], (3, C, 2 * C), (3 * C) ** -0.5, 0.1875),
        "up_weight": centred(seeds[4], (3, 3, C, CO), (9 * C) ** -0.5, 0.109375),
    }


def upsample_frame(one_frame, kernel):
    enlarged = jnp.repeat(jnp.repeat(one_frame, 2, axis=0), 2, axis=1).astype(jnp.float32)
    result = lax.conv_general_dilated(enlarged[None], kernel, (1, 1), ((1, 1), (1, 1)), dimension_numbers=('NHWC', 'HWIO', 'NHWC'), precision=lax.Precision.HIGHEST)
    return result[0].astype(jnp.bfloat16)

def reference(features, norm_gain, res_weight, time_weight, up_weight):
    values = features.astype(jnp.float32)
    inv_rms = lax.rsqrt(lax.optimization_barrier(jnp.mean(values * values, axis=-1, keepdims=True)) + 1e-06)
    activated = jax.nn.silu(values * inv_rms * norm_gain.astype(jnp.float32)).astype(jnp.bfloat16)
    branch = lax.conv_general_dilated(activated.astype(jnp.float32)[None], res_weight.astype(jnp.float32), (1, 1, 1), ((2, 0), (1, 1), (1, 1)), dimension_numbers=('NDHWC', 'DHWIO', 'NDHWC'), precision=lax.Precision.HIGHEST)[0]
    blended = (values + branch).astype(jnp.bfloat16)
    time_kernel = time_weight.astype(jnp.float32)[:, None, None]
    doubled = lax.conv_general_dilated(blended.astype(jnp.float32)[None], time_kernel, (1, 1, 1), ((2, 0), (0, 0), (0, 0)), dimension_numbers=('NDHWC', 'DHWIO', 'NDHWC'), precision=lax.Precision.HIGHEST)[0].astype(jnp.bfloat16)
    frame_count, height_in, columns, twice = doubled.shape
    channels = twice // 2
    split_up = jnp.moveaxis(doubled.reshape(frame_count, height_in, columns, 2, channels), 3, 1)
    frames_up = split_up.reshape(2 * frame_count, height_in, columns, channels)
    kernel = up_weight.astype(jnp.float32)
    return lax.map(lambda one_frame: upsample_frame(one_frame, kernel), frames_up)
```

```python
import jax
import jax.numpy as jnp
from jax import lax
from jax.experimental import pallas as pl
from jax.experimental.pallas import tpu as pltpu
from jax.sharding import PartitionSpec as P

F32 = jnp.float32
BF16 = jnp.bfloat16
VMEM = pl.BlockSpec(memory_space=pltpu.VMEM)
SMEM = pl.BlockSpec(memory_space=pltpu.SMEM)


def ring(block, axes, shift, sizes):
    total = 1
    for size in sizes:
        total *= size
    pairs = []
    for source in range(total):
        coords, rest = [], source
        for size in reversed(sizes):
            coords.insert(0, rest % size)
            rest //= size
        target = 0
        for coord, step, size in zip(coords, shift, sizes):
            target = target * size + (coord + step) % size
        pairs.append((source, target))
    return lax.ppermute(block, axes, pairs)


def activated(values, gain):
    inv = lax.rsqrt(jnp.mean(values * values, axis=-1, keepdims=True) + 1e-06)
    normed = values * inv * gain
    half = 0.5 * normed
    return half + half * jnp.tanh(half)


def residual_kernel(flags, own, prev, up, dn, pup, pdn, gain, weight, out, act):
    rows, cols, ch = own.shape[1:]
    not_first_t = flags[0].astype(F32)
    not_first_r = flags[1].astype(F32)
    not_last_r = flags[2].astype(F32)
    g = gain[...].reshape(1, 1, 1, ch)

    def put(src, frame, row, keep):
        values = src[...].astype(F32)
        a = activated(values, g)
        if keep is not None:
            a = a * keep
        act[frame : frame + 2, row : row + src.shape[1]] = a.astype(BF16)

    put(own, 2, 2, None)
    put(prev, 0, 2, not_first_t)
    put(up, 2, 0, not_first_r)
    put(dn, 2, rows + 2, not_last_r)
    put(pup, 0, 0, not_first_r * not_first_t)
    put(pdn, 0, rows + 2, not_last_r * not_first_t)

    size = 2 * (rows + 2) * cols
    acc = None
    for kt in range(3):
        lhs = jnp.concatenate(
            [act[kt : kt + 2, kh : kh + rows + 2].reshape(size, ch) for kh in range(3)], axis=1
        )
        rhs = jnp.concatenate(
            [weight[kt, :, kw].reshape(3 * ch, ch) for kw in range(3)], axis=1
        )
        part = jnp.dot(lhs, rhs, preferred_element_type=F32)
        acc = part if acc is None else acc + part
    col = lax.broadcasted_iota(jnp.int32, (size, ch), 0) % cols
    left = jnp.where(col == 0, 0.0, pltpu.roll(acc[:, :ch], 1, 0))
    right = jnp.where(col == cols - 1, 0.0, pltpu.roll(acc[:, 2 * ch :], size - 1, 0))
    branch = (left + acc[:, ch : 2 * ch] + right).reshape(2, rows + 2, cols, ch)
    out[:, 0:1] = ((up[:, 1:2].astype(F32) + branch[:, 0:1]) * not_first_r).astype(BF16)
    out[:, 1 : rows + 1] = (own[...].astype(F32) + branch[:, 1 : rows + 1]).astype(BF16)
    out[:, rows + 1 :] = ((dn[:, 0:1].astype(F32) + branch[:, rows + 1 :]) * not_last_r).astype(BF16)


def combine_kernel(weight, out):
    ch = weight.shape[2]
    w = [[weight[kh, kw].astype(F32) for kw in range(3)] for kh in range(3)]
    for phase in range(2):
        for tap in range(2):
            if phase == 0:
                r = w[0] if tap == 0 else [w[1][k] + w[2][k] for k in range(3)]
            else:
                r = [w[0][k] + w[1][k] for k in range(3)] if tap == 0 else w[2]
            row = jnp.concatenate([r[0], r[0] + r[1], r[1] + r[2], r[2]], axis=1)
            out[phase, tap * ch : (tap + 1) * ch] = row.astype(BF16)


def upsample_kernel(flags, own, prev, time_weight, up_weight, out, stack, up, woven):
    frames, rows2, cols, ch = own.shape
    rows = rows2 - 2
    stack[2:4] = own[...]
    stack[0:2] = prev[...] * flags[0].astype(BF16)
    size = frames * rows2 * cols
    lhs = jnp.concatenate([stack[k : k + 2].reshape(size, ch) for k in range(3)], axis=1)
    doubled = jnp.dot(lhs, time_weight[...].reshape(3 * ch, 2 * ch), preferred_element_type=F32)
    doubled = doubled.astype(BF16).reshape(frames, rows2, cols, 2 * ch)
    for p in range(2):
        up[:, p] = doubled[..., p * ch : (p + 1) * ch]
    co = out.shape[-1]
    ups = 2 * frames
    size = ups * rows * cols
    for phase in range(2):
        lhs = jnp.concatenate(
            [
                up[:, :, phase + tap : phase + tap + rows].reshape(size, ch)
                for tap in range(2)
            ],
            axis=1,
        )
        y = jnp.dot(lhs, up_weight[phase], preferred_element_type=F32)
        a, b = y[:, : 2 * co], y[:, 2 * co :]
        col = lax.broadcasted_iota(jnp.int32, (size, 2 * co), 0) % cols
        lane = lax.broadcasted_iota(jnp.int32, (size, 2 * co), 1)
        shift_a = jnp.where(col == 0, 0.0, pltpu.roll(a, 1, 0))
        shift_b = jnp.where(col == cols - 1, 0.0, pltpu.roll(b, size - 1, 0))
        z = jnp.where(lane < co, shift_a + b, a + shift_b)
        for parity, value in ((0, z), (1, pltpu.roll(z, co, 1))):
            for half in range(2):
                woven[half, pl.ds(parity, size, 2), :] = value[:, half * 128 : half * 128 + 128]
        for f in range(ups):
            for r in range(rows):
                at = (f * rows + r) * 2 * cols
                line = jnp.concatenate([woven[half, at : at + 2 * cols] for half in range(2)], axis=1)
                out[f, 2 * r + phase] = line[:, :co].astype(BF16)


def shards(features, norm_gain, res_weight, time_weight, up_weight):
    frames, rows, cols, ch = features.shape
    nt, nr = lax.axis_size("tm"), lax.axis_size("rows")
    co = up_weight.shape[-1]
    t, r = lax.axis_index("tm"), lax.axis_index("rows")
    flags = jnp.stack([t > 0, r > 0, r < nr - 1]).astype(jnp.int32)

    top, bottom = features[:, :2], features[:, -2:]
    axes, sizes = ("tm", "rows"), (nt, nr)
    prev = ring(features, axes, (1, 0), sizes)
    up = ring(bottom, axes, (0, 1), sizes)
    dn = ring(top, axes, (0, -1), sizes)
    pup = ring(bottom, axes, (1, 1), sizes)
    pdn = ring(top, axes, (1, -1), sizes)

    blended = pl.pallas_call(
        residual_kernel,
        out_shape=jax.ShapeDtypeStruct((2, rows + 2, cols, ch), BF16),
        in_specs=[SMEM] + [VMEM] * 8,
        out_specs=VMEM,
        scratch_shapes=[pltpu.VMEM((4, rows + 4, cols, ch), BF16)],
        compiler_params=pltpu.CompilerParams(vmem_limit_bytes=48 * 2**20),
        name="residual",
    )(flags, features, prev, up, dn, pup, pdn, norm_gain.reshape(1, ch), res_weight)

    combined = pl.pallas_call(
        combine_kernel,
        out_shape=jax.ShapeDtypeStruct((2, 2 * ch, 4 * co), BF16),
        in_specs=[VMEM],
        out_specs=VMEM,
        compiler_params=pltpu.CompilerParams(vmem_limit_bytes=32 * 2**20),
        name="combine",
    )(up_weight)

    earlier = ring(blended, axes, (1, 0), sizes)
    return pl.pallas_call(
        upsample_kernel,
        out_shape=jax.ShapeDtypeStruct((2 * frames, 2 * rows, 2 * cols, co), BF16),
        in_specs=[SMEM] + [VMEM] * 4,
        out_specs=VMEM,
        scratch_shapes=[
            pltpu.VMEM((4, rows + 2, cols, ch), BF16),
            pltpu.VMEM((2, 2, rows + 2, cols, ch), BF16),
            pltpu.VMEM((2, 2 * frames * rows * 2 * cols, 128), F32),
        ],
        compiler_params=pltpu.CompilerParams(vmem_limit_bytes=48 * 2**20),
        name="upsample",
    )(flags, blended, earlier, time_weight, combined)


def solution(mesh):
    placed = (P("tm", "rows", None, None), P(), P(), P(), P())
    return jax.shard_map(
        shards, mesh=mesh, in_specs=placed, out_specs=P("tm", "rows", None, None), check_vma=False
    )
```

```python
import jax
import jax.numpy as jnp
from jax import lax
from jax.experimental import pallas as pl
from jax.experimental.pallas import tpu as pltpu
from jax.sharding import PartitionSpec as P

F32 = jnp.float32
BF16 = jnp.bfloat16
VMEM = pl.BlockSpec(memory_space=pltpu.VMEM)
SMEM = pl.BlockSpec(memory_space=pltpu.SMEM)
HBM = pl.BlockSpec(memory_space=pltpu.HBM)


def moved(block, sizes, target):
    nt, nr = sizes
    pairs = []
    for t in range(nt):
        for r in range(nr):
            to_t, to_r = target(t, r)
            pairs.append((t * nr + r, to_t * nr + to_r))
    return lax.ppermute(block, ("tm", "rows"), pairs)


def activated(values, gain):
    inv = lax.rsqrt(jnp.mean(values * values, axis=-1, keepdims=True) + 1e-06)
    half = values * inv * gain * 0.5
    return half + half * jnp.tanh(half)


def prepare_kernel(
    features, gain, up_weight, time_weight, res_weight,
    own, act, gain_out, combined, time_out, res_out,
    gain_in, up_in, small, large,
):
    ch = own.shape[-1]
    first = [
        pltpu.make_async_copy(features, own, small.at[0]),
        pltpu.make_async_copy(gain, gain_in, small.at[1]),
        pltpu.make_async_copy(up_weight, up_in, small.at[2]),
    ]
    second = [
        pltpu.make_async_copy(res_weight.at[kt], res_out.at[kt], large.at[kt]) for kt in range(3)
    ] + [pltpu.make_async_copy(time_weight, time_out, large.at[3])]
    for copy in first + second:
        copy.start()
    for copy in first:
        copy.wait()
    g = gain_in[...].reshape(1, ch)
    gain_out[...] = g
    act[...] = activated(own[...].astype(F32), g.reshape(1, 1, 1, ch)).astype(BF16)
    w = [[up_in[kh, kw].astype(F32) for kw in range(3)] for kh in range(3)]
    for phase in range(2):
        for tap in range(2):
            if phase == 0:
                r = w[0] if tap == 0 else [w[1][k] + w[2][k] for k in range(3)]
            else:
                r = [w[0][k] + w[1][k] for k in range(3)] if tap == 0 else w[2]
            block = jnp.concatenate([r[0], r[0] + r[1], r[1] + r[2], r[2]], axis=0)
            combined[phase, tap * ch : (tap + 1) * ch] = block.T.astype(BF16)
    for copy in second:
        copy.wait()


def columns_summed(acc, cols, ch):
    size = acc.shape[0]
    col = lax.broadcasted_iota(jnp.int32, (size, ch), 0) % cols
    left = jnp.where(col == 0, 0.0, pltpu.roll(acc[:, :ch], 1, 0))
    right = jnp.where(col == cols - 1, 0.0, pltpu.roll(acc[:, 2 * ch :], size - 1, 0))
    return left + acc[:, ch : 2 * ch] + right


def taps(windows, weight, first, count):
    ch = weight.shape[-1]
    lhs = jnp.concatenate(windows, axis=1)
    rhs = jnp.concatenate(
        [weight[first : first + count, :, kw].reshape(count * 3 * ch, ch) for kw in range(3)], axis=1
    )
    return jnp.dot(lhs, rhs, preferred_element_type=F32)


def inner_kernel(flags, act_own, own, prev, gain, weight, out, act_rim, act):
    rows, cols, ch = own.shape[1:]
    act[2:4] = act_own[...]
    keep = flags[0].astype(F32)
    act[0:2] = (activated(prev[...].astype(F32), gain[...].reshape(1, 1, 1, ch)) * keep).astype(BF16)
    act_rim[:, 0] = act[:, 0:2]
    act_rim[:, 1] = act[:, rows - 2 : rows]
    lines = rows - 2

    windows = [
        act[kt : kt + 2, kh : kh + lines].reshape(2 * lines * cols, ch)
        for kt in range(3)
        for kh in range(3)
    ]
    branch = columns_summed(taps(windows, weight, 0, 3), cols, ch).reshape(2, lines, cols, ch)
    out[...] = (own[:, 1 : rows - 1].astype(F32) + branch).astype(BF16)


def halo_kernel(flags, pair, cross, gain, out):
    ch = pair.shape[-1]
    odd = flags[3]
    inside = jnp.where(odd == 1, flags[2], flags[1]).astype(F32)
    g = gain[...].reshape(1, 1, 1, ch)
    out[:, 1 - odd] = activated(pair[...].astype(F32), g).astype(BF16)
    out[:, odd] = (activated(cross[...].astype(F32), g) * inside).astype(BF16)


def rim_windows(act, start, count, cols, ch):
    return [
        act[start : start + count, :, kh : kh + 2].reshape(count * 4 * cols, ch) for kh in range(3)
    ]


def rim_own_kernel(flags, act_rim, halo, own, pair, cross, weight, out, act):
    rows, cols, ch = own.shape[1:]
    odd = flags[3]
    act[:, 0, 0:2] = halo[:, 0]
    act[:, 0, 2:4] = act_rim[2:4, 0]
    act[:, 1, 0:2] = act_rim[2:4, 1]
    act[:, 1, 2:4] = halo[:, 1]
    both = taps(rim_windows(act, 0, 2, cols, ch), weight, 2, 1)
    late = taps(rim_windows(act, 0, 1, cols, ch), weight, 1, 1)
    half = late.shape[0]
    acc = jnp.concatenate([both[:half], both[half:] + late], axis=0)
    branch = columns_summed(acc, cols, ch).reshape(2, 2, 2, cols, ch)
    out[:, 0, 1] = own[:, 0].astype(F32) + branch[:, 0, 1]
    out[:, 1, 0] = own[:, rows - 1].astype(F32) + branch[:, 1, 0]
    above = jnp.where(odd == 1, pair[:, 1].astype(F32), cross[:, 1].astype(F32))
    below = jnp.where(odd == 1, cross[:, 0].astype(F32), pair[:, 0].astype(F32))
    out[:, 0, 0] = above + branch[:, 0, 0]
    out[:, 1, 1] = below + branch[:, 1, 1]


def rim_kernel(flags, act_rim, halo, partial, weight, out, act):
    cols, ch = partial.shape[3:]
    keep = flags[0].astype(BF16)
    act[:, 0, 0:2] = halo[:, 0] * keep
    act[:, 0, 2:4] = act_rim[0:2, 0]
    act[:, 1, 0:2] = act_rim[0:2, 1]
    act[:, 1, 2:4] = halo[:, 1] * keep
    both = taps(rim_windows(act, 0, 2, cols, ch), weight, 0, 1)
    early = taps(rim_windows(act, 1, 1, cols, ch), weight, 1, 1)
    half = early.shape[0]
    acc = jnp.concatenate([both[:half] + early, both[half:]], axis=0)
    blended = partial[...] + columns_summed(acc, cols, ch).reshape(2, 2, 2, cols, ch)
    out[:, 0, 0] = (blended[:, 0, 0] * flags[1].astype(F32)).astype(BF16)
    out[:, 0, 1] = blended[:, 0, 1].astype(BF16)
    out[:, 1, 0] = blended[:, 1, 0].astype(BF16)
    out[:, 1, 1] = (blended[:, 1, 1] * flags[2].astype(F32)).astype(BF16)


def time_upsampled(own, prev, keep, time_weight, stack):
    frames, lines, cols, ch = own.shape
    stack[2:4] = own
    stack[0:2] = prev * keep
    size = frames * lines * cols
    lhs = jnp.concatenate([stack[k : k + 2].reshape(size, ch) for k in range(3)], axis=1)
    doubled = jnp.dot(lhs, time_weight[...].reshape(3 * ch, 2 * ch), preferred_element_type=F32)
    return doubled.astype(BF16).reshape(frames, lines, cols, 2 * ch)


def woven_columns(upper, lower, weight, woven, cols, co):
    y = jnp.dot(jnp.concatenate([upper, lower], axis=1), weight, preferred_element_type=F32)
    size = y.shape[0]
    a, b = y[:, : 2 * co], y[:, 2 * co :]
    col = lax.broadcasted_iota(jnp.int32, (size, 2 * co), 0) % cols
    lane = lax.broadcasted_iota(jnp.int32, (size, 2 * co), 1)
    shift_a = jnp.where(col == 0, 0.0, pltpu.roll(a, 1, 0))
    shift_b = jnp.where(col == cols - 1, 0.0, pltpu.roll(b, size - 1, 0))
    z = jnp.where(lane < co, shift_a + b, a + shift_b)
    for parity, value in ((0, z), (1, pltpu.roll(z, co, 1))):
        for half in range(2):
            woven[half, pl.ds(parity, size, 2), :] = value[:, half * 128 : half * 128 + 128]

    def line(index):
        at = index * 2 * cols
        both = jnp.concatenate([woven[half, at : at + 2 * cols] for half in range(2)], axis=1)
        return both[:, :co].astype(BF16)

    return line


def up_inner_kernel(flags, own, prev, time_weight, weight, out, rim, stack, up, woven, stage, sem):
    frames, lines, cols, ch = own.shape
    co = out.shape[-1]
    keep = flags[0].astype(BF16)
    doubled = time_upsampled(own[...], prev[...], keep, time_weight, stack)
    for p in range(2):
        up[:, p] = doubled[..., p * ch : (p + 1) * ch]
    for p in range(2):
        rim[:, p, 0] = up[:, p, 0]
        rim[:, p, 1] = up[:, p, lines - 1]
    pairs = lines - 1
    size = 2 * frames * pairs * cols
    upper = up[:, :, 0:pairs].reshape(size, ch)
    lower = up[:, :, 1 : pairs + 1].reshape(size, ch)
    for phase in range(2):
        line = woven_columns(upper, lower, weight[phase], woven, cols, co)
        for f in range(2 * frames):
            for j in range(pairs):
                stage[f, 2 * j + 1 - phase] = line(f * pairs + j)
    copy = pltpu.make_async_copy(stage, out.at[:, 3 : 3 + 2 * pairs], sem)
    copy.start()
    copy.wait()


def up_rim_kernel(
    flags, own, prev, inner, time_weight, weight, partial, out, stack, up, woven, stage, sems
):
    del partial
    frames, sides, lines, cols, ch = own.shape
    co = out.shape[-1]
    keep = flags[0].astype(BF16)
    flat = (frames, sides * lines, cols, ch)
    doubled = time_upsampled(own[...].reshape(flat), prev[...].reshape(flat), keep, time_weight, stack)
    for p in range(2):
        part = doubled[..., p * ch : (p + 1) * ch]
        up[:, p, 0, 0:2] = part[:, 0:2]
        up[:, p, 1, 1:3] = part[:, 2:4]
        up[:, p, 0, 2] = inner[:, p, 0]
        up[:, p, 1, 0] = inner[:, p, 1]
    size = 2 * frames * 3 * cols
    last = out.shape[1] - 3
    for phase in range(2):
        picks = ((0, 0, 0), (0, 1, 2), (1, 0, 1)) if phase == 0 else ((0, 1, 1), (1, 0, 0), (1, 1, 2))

        def taken(step):
            lines_taken = [up[:, :, s, i + step : i + step + 1] for s, i, _ in picks]
            return jnp.concatenate(lines_taken, axis=2).reshape(size, ch)

        line = woven_columns(taken(0), taken(1), weight[phase], woven, cols, co)
        for f in range(2 * frames):
            for j, (s, _, at) in enumerate(picks):
                stage[s, f, at] = line(f * 3 + j)
    copies = [
        pltpu.make_async_copy(stage.at[s], out.at[:, start : start + 3], sems.at[s])
        for s, start in ((0, 0), (1, last))
    ]
    for copy in copies:
        copy.start()
    for copy in copies:
        copy.wait()


def call(kernel, name, shapes, specs, scratch, mib, args, in_out=None, out_specs=None, us=1):
    several = isinstance(shapes, list)
    return pl.pallas_call(
        kernel,
        out_shape=shapes,
        in_specs=specs,
        out_specs=out_specs if out_specs is not None else ([VMEM] * len(shapes) if several else VMEM),
        scratch_shapes=scratch,
        compiler_params=pltpu.CompilerParams(vmem_limit_bytes=mib * 2**20),
        cost_estimate=pl.CostEstimate(flops=us * 10**9, bytes_accessed=us * 3 * 10**9 // 1000, transcendentals=0),
        input_output_aliases=in_out or {},
        name=name,
    )(*args)


def vmem_out(shape, dtype):
    return pltpu.VMEM(shape, dtype)


def in_hbm(array):
    return pltpu.with_memory_space_constraint(array, pltpu.HBM)


def in_vmem(array):
    return pltpu.with_memory_space_constraint(array, pltpu.VMEM)


def shards(features, norm_gain, res_weight, time_weight, up_weight):
    frames, rows, cols, ch = features.shape
    nt, nr = lax.axis_size("tm"), lax.axis_size("rows")
    co = up_weight.shape[-1]
    t, r = lax.axis_index("tm"), lax.axis_index("rows")
    flags = jnp.stack([t > 0, r > 0, r < nr - 1, (r & 1) == 1]).astype(jnp.int32)
    sizes = (nt, nr)
    shape = jax.ShapeDtypeStruct

    def paired(r):
        return r ^ 1

    def crossed(r):
        return min(max((r + 1 ^ 1) - 1, 0), nr - 1)

    def later(block):
        return moved(block, sizes, lambda t, r: ((t + 1) % nt, r))

    prev = later(features)
    odd = (r & 1) == 1
    top, bottom = features[:, :2], features[:, -2:]
    to_pair = jnp.where(odd, top, bottom)
    to_cross = jnp.where(odd, bottom, top)
    cross = moved(to_cross, sizes, lambda t, r: (t, crossed(r)))
    pair = moved(to_pair, sizes, lambda t, r: (t, paired(r)))
    up_turned = jnp.swapaxes(up_weight, 2, 3)
    own, act_own, gain, combined, time_held, res_held = call(
        prepare_kernel,
        "prepare",
        [
            vmem_out(features.shape, BF16),
            vmem_out(features.shape, BF16),
            vmem_out((1, ch), F32),
            vmem_out((2, 2 * ch, 4 * co), BF16),
            vmem_out(time_weight.shape, BF16),
            vmem_out(res_weight.shape, BF16),
        ],
        [HBM] * 5,
        [
            pltpu.VMEM((ch,), F32),
            pltpu.VMEM(up_turned.shape, BF16),
            pltpu.SemaphoreType.DMA((3,)),
            pltpu.SemaphoreType.DMA((4,)),
        ],
        24,
        tuple(in_hbm(a) for a in (features, norm_gain, up_turned, time_weight, res_weight)),
    )
    halo = call(
        halo_kernel,
        "halo",
        vmem_out((2, 2, 2, cols, ch), BF16),
        [SMEM] + [VMEM] * 3,
        [],
        8,
        (flags, pair, cross, gain),
    )
    prev_halo = later(halo)
    lines = rows - 2
    inner, act_rim = call(
        inner_kernel,
        "inner",
        [shape((2, lines, cols, ch), BF16), shape((4, 2, 2, cols, ch), BF16)],
        [SMEM] + [VMEM] * 5,
        [pltpu.VMEM((4, rows, cols, ch), BF16)],
        16,
        (flags, act_own, own, prev, gain, in_vmem(res_held)),
    )
    inner_prev = later(inner)
    side_rows = [pltpu.VMEM((2, 2, 4, cols, ch), BF16)]
    rim_own = call(
        rim_own_kernel,
        "rim_own",
        vmem_out((2, 2, 2, cols, ch), F32),
        [SMEM] + [VMEM] * 6,
        side_rows,
        16,
        (flags, act_rim, halo, own, pair, cross, in_vmem(res_held)),
    )
    rim = call(
        rim_kernel,
        "rim",
        shape((2, 2, 2, cols, ch), BF16),
        [SMEM] + [VMEM] * 4,
        side_rows,
        16,
        (flags, act_rim, prev_halo, rim_own, in_vmem(res_held)),
    )
    rim_prev = later(rim)
    out_shape = shape((2 * frames, 2 * rows, 2 * cols, co), BF16)
    partial, up_rim = call(
        up_inner_kernel,
        "up_inner",
        [out_shape, shape((2, 2, 2, cols, ch), BF16)],
        [SMEM] + [VMEM] * 4,
        [
            pltpu.VMEM((4, lines, cols, ch), BF16),
            pltpu.VMEM((2, 2, lines, cols, ch), BF16),
            pltpu.VMEM((2, 2 * frames * (lines - 1) * 2 * cols, 128), F32),
            pltpu.VMEM((2 * frames, 2 * (lines - 1), 2 * cols, co), BF16),
            pltpu.SemaphoreType.DMA,
        ],
        24,
        (flags, inner, inner_prev, in_vmem(time_held), in_vmem(combined)),
        out_specs=[HBM, VMEM],
    )
    return call(
        up_rim_kernel,
        "up_rim",
        out_shape,
        [SMEM] + [VMEM] * 5 + [HBM],
        [
            pltpu.VMEM((4, 4, cols, ch), BF16),
            pltpu.VMEM((2, 2, 2, 3, cols, ch), BF16),
            pltpu.VMEM((2, 2 * frames * 3 * 2 * cols, 128), F32),
            pltpu.VMEM((2, 2 * frames, 3, 2 * cols, co), BF16),
            pltpu.SemaphoreType.DMA((2,)),
        ],
        24,
        (flags, rim, rim_prev, up_rim, in_vmem(time_held), in_vmem(combined), partial),
        in_out={6: 0},
        out_specs=HBM,
    )


def solution(mesh):
    placed = (P("tm", "rows", None, None), P(), P(), P(), P())
    return jax.shard_map(
        shards, mesh=mesh, in_specs=placed, out_specs=P("tm", "rows", None, None), check_vma=False
    )
```

```python
import jax
import jax.numpy as jnp
from jax import lax
from jax.experimental import pallas as pl
from jax.experimental.pallas import tpu as pltpu
from jax.sharding import PartitionSpec as P

F32 = jnp.float32
BF16 = jnp.bfloat16
VMEM = pl.BlockSpec(memory_space=pltpu.VMEM)
SMEM = pl.BlockSpec(memory_space=pltpu.SMEM)
HBM = pl.BlockSpec(memory_space=pltpu.HBM)


def moved(block, sizes, target):
    nt, nr = sizes
    pairs = []
    for t in range(nt):
        for r in range(nr):
            to_t, to_r = target(t, r)
            pairs.append((t * nr + r, to_t * nr + to_r))
    return lax.ppermute(block, ("tm", "rows"), pairs)


def activated(values, gain):
    inv = lax.rsqrt(jnp.mean(values * values, axis=-1, keepdims=True) + 1e-06)
    half = values * inv * gain * 0.5
    return half + half * jnp.tanh(half)


def inner_windows(act, start, count, cols, ch):
    lines = act.shape[1] - 2
    return [
        act[start : start + count, kh : kh + lines].reshape(count * lines * cols, ch)
        for kh in range(3)
    ]


def prepare_kernel(
    features, gain, res_weight, own, act, gain_out, res_held, partial, gain_in, sems
):
    rows, cols, ch = own.shape[1:]
    copies = [
        pltpu.make_async_copy(source, target, sems.at[i])
        for i, (source, target) in enumerate(
            ((gain, gain_in), (features, own))
            + tuple((res_weight.at[kt], res_held.at[kt]) for kt in (2, 1, 0))
        )
    ]
    for copy in copies:
        copy.start()
    copies[0].wait()
    copies[1].wait()
    g = gain_in[...].reshape(1, ch)
    gain_out[...] = g
    act[...] = activated(own[...].astype(F32), g.reshape(1, 1, 1, ch)).astype(BF16)
    copies[2].wait()
    both = taps(inner_windows(act, 0, 2, cols, ch), res_held.at[2])
    copies[3].wait()
    late = taps(inner_windows(act, 0, 1, cols, ch), res_held.at[1])
    half = late.shape[0]
    acc = jnp.concatenate([both[:half], both[half:] + late], axis=0)
    branch = columns_summed(acc, cols, ch).reshape(2, rows - 2, cols, ch)
    partial[...] = own[:, 1 : rows - 1].astype(F32) + branch
    copies[4].wait()


def combine_kernel(up_weight, time_weight, after, combined, time_out, up_in, sems):
    del after
    ch = time_out.shape[1]
    copies = [
        pltpu.make_async_copy(source, target, sems.at[i])
        for i, (source, target) in enumerate(((up_weight, up_in), (time_weight, time_out)))
    ]
    for copy in copies:
        copy.start()
    copies[0].wait()
    w = [[up_in[kh, kw].astype(F32) for kw in range(3)] for kh in range(3)]
    for phase in range(2):
        for tap in range(2):
            if phase == 0:
                r = w[0] if tap == 0 else [w[1][k] + w[2][k] for k in range(3)]
            else:
                r = [w[0][k] + w[1][k] for k in range(3)] if tap == 0 else w[2]
            block = jnp.concatenate([r[0], r[0] + r[1], r[1] + r[2], r[2]], axis=0)
            combined[phase, tap * ch : (tap + 1) * ch] = block.T.astype(BF16)
    copies[1].wait()


def columns_summed(acc, cols, ch):
    size = acc.shape[0]
    col = lax.broadcasted_iota(jnp.int32, (size, ch), 0) % cols
    left = jnp.where(col == 0, 0.0, pltpu.roll(acc[:, :ch], 1, 0))
    right = jnp.where(col == cols - 1, 0.0, pltpu.roll(acc[:, 2 * ch :], size - 1, 0))
    return left + acc[:, ch : 2 * ch] + right


def taps(windows, weight):
    ch = weight.shape[-1]
    lhs = jnp.concatenate(windows, axis=1)
    rhs = jnp.concatenate([weight[:, kw].reshape(3 * ch, ch) for kw in range(3)], axis=1)
    return jnp.dot(lhs, rhs, preferred_element_type=F32)


def inner_kernel(flags, prev, gain, res_held, partial, out, act):
    rows, cols, ch = act.shape[1:]
    keep = flags[0].astype(F32)
    act[...] = (activated(prev[...].astype(F32), gain[...].reshape(1, 1, 1, ch)) * keep).astype(BF16)
    both = taps(inner_windows(act, 0, 2, cols, ch), res_held.at[0])
    early = taps(inner_windows(act, 1, 1, cols, ch), res_held.at[1])
    half = early.shape[0]
    acc = jnp.concatenate([both[:half] + early, both[half:]], axis=0)
    branch = columns_summed(acc, cols, ch).reshape(2, rows - 2, cols, ch)
    out[...] = (partial[...] + branch).astype(BF16)


def halo_kernel(flags, cross, pair, gain, out):
    ch = pair.shape[-1]
    odd = flags[3]
    inside = jnp.where(odd == 1, flags[2], flags[1]).astype(F32)
    g = gain[...].reshape(1, 1, 1, ch)
    out[:, 1 - odd] = activated(pair[...].astype(F32), g).astype(BF16)
    out[:, odd] = (activated(cross[...].astype(F32), g) * inside).astype(BF16)


def rim_windows(act, start, count, cols, ch):
    return [
        act[start : start + count, :, kh : kh + 2].reshape(count * 4 * cols, ch) for kh in range(3)
    ]


def rim_own_kernel(flags, act_own, halo, own, cross, pair, res_held, out, act):
    rows, cols, ch = own.shape[1:]
    odd = flags[3]
    act[:, 0, 0:2] = halo[:, 0]
    act[:, 0, 2:4] = act_own[:, 0:2]
    act[:, 1, 0:2] = act_own[:, rows - 2 : rows]
    act[:, 1, 2:4] = halo[:, 1]
    both = taps(rim_windows(act, 0, 2, cols, ch), res_held.at[2])
    late = taps(rim_windows(act, 0, 1, cols, ch), res_held.at[1])
    half = late.shape[0]
    acc = jnp.concatenate([both[:half], both[half:] + late], axis=0)
    branch = columns_summed(acc, cols, ch).reshape(2, 2, 2, cols, ch)
    out[:, 0, 1] = own[:, 0].astype(F32) + branch[:, 0, 1]
    out[:, 1, 0] = own[:, rows - 1].astype(F32) + branch[:, 1, 0]
    above = jnp.where(odd == 1, pair[:, 1].astype(F32), cross[:, 1].astype(F32))
    below = jnp.where(odd == 1, cross[:, 0].astype(F32), pair[:, 0].astype(F32))
    out[:, 0, 0] = above + branch[:, 0, 0]
    out[:, 1, 1] = below + branch[:, 1, 1]


def rim_kernel(flags, act_prev, halo, partial, res_held, out, act):
    rows = act_prev.shape[1]
    cols, ch = partial.shape[3:]
    keep = flags[0].astype(BF16)
    act[:, 0, 0:2] = halo[:, 0] * keep
    act[:, 0, 2:4] = act_prev[:, 0:2]
    act[:, 1, 0:2] = act_prev[:, rows - 2 : rows]
    act[:, 1, 2:4] = halo[:, 1] * keep
    both = taps(rim_windows(act, 0, 2, cols, ch), res_held.at[0])
    early = taps(rim_windows(act, 1, 1, cols, ch), res_held.at[1])
    half = early.shape[0]
    acc = jnp.concatenate([both[:half] + early, both[half:]], axis=0)
    blended = partial[...] + columns_summed(acc, cols, ch).reshape(2, 2, 2, cols, ch)
    out[:, 0, 0] = (blended[:, 0, 0] * flags[1].astype(F32)).astype(BF16)
    out[:, 0, 1] = blended[:, 0, 1].astype(BF16)
    out[:, 1, 0] = blended[:, 1, 0].astype(BF16)
    out[:, 1, 1] = (blended[:, 1, 1] * flags[2].astype(F32)).astype(BF16)


def time_products(windows, weight, first):
    ch = weight.shape[1]
    count = len(windows)
    lhs = jnp.concatenate(windows, axis=1) if count > 1 else windows[0]
    rhs = weight[first : first + count].reshape(count * ch, 2 * ch)
    return jnp.dot(lhs, rhs, preferred_element_type=F32)


def woven_columns(upper, lower, weight, woven, cols, co):
    y = jnp.dot(jnp.concatenate([upper, lower], axis=1), weight, preferred_element_type=F32)
    size = y.shape[0]
    a, b = y[:, : 2 * co], y[:, 2 * co :]
    col = lax.broadcasted_iota(jnp.int32, (size, 2 * co), 0) % cols
    lane = lax.broadcasted_iota(jnp.int32, (size, 2 * co), 1)
    shift_a = jnp.where(col == 0, 0.0, pltpu.roll(a, 1, 0))
    shift_b = jnp.where(col == cols - 1, 0.0, pltpu.roll(b, size - 1, 0))
    z = jnp.where(lane < co, shift_a + b, a + shift_b)
    for parity, value in ((0, z), (1, pltpu.roll(z, co, 1))):
        for half in range(2):
            woven[half, pl.ds(parity, size, 2), :] = value[:, half * 128 : half * 128 + 128]

    def line(index):
        at = index * 2 * cols
        both = jnp.concatenate([woven[half, at : at + 2 * cols] for half in range(2)], axis=1)
        return both[:, :co].astype(BF16)

    return line


def up_inner_kernel(flags, own, prev, rim_own, time_weight, weight, stage, inner_rim, rim_part, stack, up, woven):
    frames, lines, cols, ch = own.shape
    co = stage.shape[-1]
    stack[2:4] = own[...]
    stack[0:2] = prev[...] * flags[0].astype(BF16)
    size = frames * lines * cols
    windows = [stack[k : k + 2].reshape(size, ch) for k in range(3)]
    doubled = time_products(windows, time_weight, 0).astype(BF16).reshape(frames, lines, cols, 2 * ch)
    for p in range(2):
        up[:, p] = doubled[..., p * ch : (p + 1) * ch]
    for p in range(2):
        inner_rim[:, p, 0] = up[:, p, 0]
        inner_rim[:, p, 1] = up[:, p, lines - 1]
    pairs = lines - 1
    size = 2 * frames * pairs * cols
    upper = up[:, :, 0:pairs].reshape(size, ch)
    lower = up[:, :, 1 : pairs + 1].reshape(size, ch)
    for phase in range(2):
        line = woven_columns(upper, lower, weight[phase], woven, cols, co)
        for f in range(2 * frames):
            for j in range(pairs):
                stage[f, 2 * j + 1 - phase] = line(f * pairs + j)
    half = rim_own.shape[1] * rim_own.shape[2] * cols
    first = rim_own[0].reshape(half, ch)
    rim_part[0:half] = time_products([first], time_weight, 2)
    rim_part[half:] = time_products([first, rim_own[1].reshape(half, ch)], time_weight, 1)


def up_rim_kernel(
    flags, part, prev, inner_rim, inner_stage, time_weight, weight, out, up, woven, stage, sems
):
    frames, sides, lines, cols, ch = prev.shape
    co = out.shape[-1]
    middle = pltpu.make_async_copy(inner_stage, out.at[:, 3 : 3 + inner_stage.shape[1]], sems.at[6])
    middle.start()
    keep = flags[0].astype(BF16)
    half = sides * lines * cols
    before = prev[0].reshape(half, ch) * keep
    last = prev[1].reshape(half, ch) * keep
    products = (
        part[0:half] + time_products([before, last], time_weight, 0),
        part[half:] + time_products([last], time_weight, 0),
    )
    for frame in range(frames):
        doubled = products[frame].astype(BF16).reshape(sides * lines, cols, 2 * ch)
        for p in range(2):
            lot = doubled[..., p * ch : (p + 1) * ch]
            up[frame, p, 0, 0:2] = lot[0:2]
            up[frame, p, 1, 1:3] = lot[2:4]
            up[frame, p, 0, 2] = inner_rim[frame, p, 0]
            up[frame, p, 1, 0] = inner_rim[frame, p, 1]
    size = 2 * frames * 3 * cols
    start = out.shape[1] - 3
    copies = [middle]
    for phase in range(2):
        if phase == 0:
            picks = ((0, 0, 0), (0, 1, 2), (1, 0, start + 1))
        else:
            picks = ((0, 1, 1), (1, 0, start), (1, 1, start + 2))

        def taken(step):
            lines_taken = [up[:, :, s, i + step : i + step + 1] for s, i, _ in picks]
            return jnp.concatenate(lines_taken, axis=2).reshape(size, ch)

        line = woven_columns(taken(0), taken(1), weight[phase], woven, cols, co)
        for j, (_, _, row) in enumerate(picks):
            for f in range(2 * frames):
                stage[phase, j, f, 0] = line(f * 3 + j)
            copy = pltpu.make_async_copy(
                stage.at[phase, j], out.at[:, row : row + 1], sems.at[phase * 3 + j]
            )
            copy.start()
            copies.append(copy)
    for copy in copies:
        copy.wait()


def call(kernel, name, shapes, specs, scratch, mib, args, out_specs=None, us=1):
    several = isinstance(shapes, list)
    return pl.pallas_call(
        kernel,
        out_shape=shapes,
        in_specs=specs,
        out_specs=out_specs if out_specs is not None else ([VMEM] * len(shapes) if several else VMEM),
        scratch_shapes=scratch,
        compiler_params=pltpu.CompilerParams(vmem_limit_bytes=mib * 2**20),
        cost_estimate=pl.CostEstimate(flops=us * 10**9, bytes_accessed=us * 3 * 10**9 // 1000, transcendentals=0),
        name=name,
    )(*args)


def vmem_out(shape, dtype):
    return pltpu.VMEM(shape, dtype)


def in_hbm(array):
    return pltpu.with_memory_space_constraint(array, pltpu.HBM)


def in_vmem(array):
    return pltpu.with_memory_space_constraint(array, pltpu.VMEM)


def shards(features, norm_gain, res_weight, time_weight, up_weight):
    frames, rows, cols, ch = features.shape
    nt, nr = lax.axis_size("tm"), lax.axis_size("rows")
    co = up_weight.shape[-1]
    t, r = lax.axis_index("tm"), lax.axis_index("rows")
    flags = jnp.stack([t > 0, r > 0, r < nr - 1, (r & 1) == 1]).astype(jnp.int32)
    sizes = (nt, nr)
    shape = jax.ShapeDtypeStruct

    def paired(r):
        return r ^ 1

    def crossed(r):
        return min(max((r + 1 ^ 1) - 1, 0), nr - 1)

    def later(block):
        return moved(block, sizes, lambda t, r: ((t + 1) % nt, r))

    odd = (r & 1) == 1
    top, bottom = features[:, :2], features[:, -2:]
    to_pair = jnp.where(odd, top, bottom)
    to_cross = jnp.where(odd, bottom, top)
    to_cross, to_pair, sent = lax.optimization_barrier((to_cross, to_pair, features))
    prev = later(sent)
    cross = moved(to_cross, sizes, lambda t, r: (t, crossed(r)))
    pair = moved(to_pair, sizes, lambda t, r: (t, paired(r)))
    own, act_own, gain, res_held, inner_own = call(
        prepare_kernel,
        "prepare",
        [
            vmem_out(features.shape, BF16),
            vmem_out(features.shape, BF16),
            vmem_out((1, ch), F32),
            vmem_out(res_weight.shape, BF16),
            vmem_out((2, rows - 2, cols, ch), F32),
        ],
        [HBM] * 3,
        [pltpu.VMEM((ch,), F32), pltpu.SemaphoreType.DMA((5,))],
        16,
        tuple(in_hbm(a) for a in (features, norm_gain, res_weight)),
    )
    lines = rows - 2
    halo = call(
        halo_kernel,
        "halo",
        vmem_out((2, 2, 2, cols, ch), BF16),
        [SMEM] + [VMEM] * 3,
        [],
        8,
        (flags, cross, pair, gain),
    )
    prev_halo = later(halo)
    act_prev_shape = vmem_out((2, rows, cols, ch), BF16)
    inner, act_prev = call(
        inner_kernel,
        "inner",
        [shape((2, lines, cols, ch), BF16), act_prev_shape],
        [SMEM] + [VMEM] * 4,
        [],
        16,
        (flags, prev, gain, in_vmem(res_held), inner_own),
    )
    inner_prev = later(inner)
    side_rows = [pltpu.VMEM((2, 2, 4, cols, ch), BF16)]
    rim_own = call(
        rim_own_kernel,
        "rim_own",
        vmem_out((2, 2, 2, cols, ch), F32),
        [SMEM] + [VMEM] * 6,
        side_rows,
        16,
        (flags, act_own, halo, own, cross, pair, in_vmem(res_held)),
    )
    rim = call(
        rim_kernel,
        "rim",
        shape((2, 2, 2, cols, ch), BF16),
        [SMEM] + [VMEM] * 4,
        side_rows,
        16,
        (flags, act_prev, prev_halo, rim_own, in_vmem(res_held)),
    )
    rim_prev = later(rim)
    up_turned = jnp.swapaxes(up_weight, 2, 3)
    combined, time_held = call(
        combine_kernel,
        "combine",
        [vmem_out((2, 2 * ch, 4 * co), BF16), vmem_out(time_weight.shape, BF16)],
        [HBM] * 2 + [VMEM],
        [pltpu.VMEM(up_turned.shape, BF16), pltpu.SemaphoreType.DMA((2,))],
        16,
        (in_hbm(up_turned), in_hbm(time_weight), rim),
    )
    stage, inner_rim, rim_part = call(
        up_inner_kernel,
        "up_inner",
        [
            vmem_out((2 * frames, 2 * (lines - 1), 2 * cols, co), BF16),
            vmem_out((2, 2, 2, cols, ch), BF16),
            vmem_out((frames * 4 * cols, 2 * ch), F32),
        ],
        [SMEM] + [VMEM] * 5,
        [
            pltpu.VMEM((4, lines, cols, ch), BF16),
            pltpu.VMEM((2, 2, lines, cols, ch), BF16),
            pltpu.VMEM((2, 2 * frames * (lines - 1) * 2 * cols, 128), F32),
        ],
        24,
        (flags, inner, inner_prev, rim, in_vmem(time_held), in_vmem(combined)),
    )
    return call(
        up_rim_kernel,
        "up_rim",
        shape((2 * frames, 2 * rows, 2 * cols, co), BF16),
        [SMEM] + [VMEM] * 6,
        [
            pltpu.VMEM((2, 2, 2, 3, cols, ch), BF16),
            pltpu.VMEM((2, 2 * frames * 3 * 2 * cols, 128), F32),
            pltpu.VMEM((2, 3, 2 * frames, 1, 2 * cols, co), BF16),
            pltpu.SemaphoreType.DMA((7,)),
        ],
        24,
        (flags, rim_part, rim_prev, inner_rim, stage, in_vmem(time_held), in_vmem(combined)),
        out_specs=HBM,
    )


def solution(mesh):
    placed = (P("tm", "rows", None, None), P(), P(), P(), P())
    return jax.shard_map(
        shards, mesh=mesh, in_specs=placed, out_specs=P("tm", "rows", None, None), check_vma=False
    )
```

```python
import functools

import jax
import jax.numpy as jnp
from jax import lax
from jax.experimental import pallas as pl
from jax.experimental.pallas import tpu as pltpu
from jax.sharding import PartitionSpec as P

F32 = jnp.float32
BF16 = jnp.bfloat16
VMEM = pl.BlockSpec(memory_space=pltpu.VMEM)
SMEM = pl.BlockSpec(memory_space=pltpu.SMEM)
HBM = pl.BlockSpec(memory_space=pltpu.HBM)


def moved(block, sizes, target):
    nt, nr = sizes
    pairs = []
    for t in range(nt):
        for r in range(nr):
            to_t, to_r = target(t, r)
            pairs.append((t * nr + r, to_t * nr + to_r))
    return lax.ppermute(block, ("tm", "rows"), pairs)


def activated(values, gain):
    inv = lax.rsqrt(jnp.mean(values * values, axis=-1, keepdims=True) + 1e-06)
    half = values * inv * gain * 0.5
    return half + half * jnp.tanh(half)


def inner_windows(act, start, count, cols, ch):
    lines = act.shape[1] - 2
    return [
        act[start : start + count, kh : kh + lines].reshape(count * lines * cols, ch)
        for kh in range(3)
    ]


def parity_kernel(flags, out):
    out[...] = jnp.zeros(out.shape, F32) + flags[3].astype(F32)


def prepare_kernel(
    features, gain, up_weight, time_weight, res_held,
    own, act, gain_out, partial, up_out, time_out,
    gain_in, sems,
):
    rows, cols, ch = own.shape[1:]
    copies = [
        pltpu.make_async_copy(source, target, sems.at[i])
        for i, (source, target) in enumerate(
            ((gain, gain_in), (features, own), (up_weight, up_out), (time_weight, time_out))
        )
    ]
    for copy in copies:
        copy.start()
    copies[0].wait()
    copies[1].wait()
    g = gain_in[...].reshape(1, ch)
    gain_out[...] = g
    act[...] = activated(own[...].astype(F32), g.reshape(1, 1, 1, ch)).astype(BF16)
    both = taps(inner_windows(act, 0, 2, cols, ch), res_held.at[2])
    late = taps(inner_windows(act, 0, 1, cols, ch), res_held.at[1])
    half = late.shape[0]
    acc = jnp.concatenate([both[:half], both[half:] + late], axis=0)
    branch = columns_summed(acc, cols, ch).reshape(2, rows - 2, cols, ch)
    partial[...] = own[:, 1 : rows - 1].astype(F32) + branch
    copies[2].wait()
    copies[3].wait()


def combine(up_weight, combined):
    ch = up_weight.shape[-1]
    w = [[up_weight[kh, kw].astype(F32) for kw in range(3)] for kh in range(3)]
    for phase in range(2):
        for tap in range(2):
            if phase == 0:
                r = w[0] if tap == 0 else [w[1][k] + w[2][k] for k in range(3)]
            else:
                r = [w[0][k] + w[1][k] for k in range(3)] if tap == 0 else w[2]
            block = jnp.concatenate([r[0], r[0] + r[1], r[1] + r[2], r[2]], axis=0)
            combined[phase, tap * ch : (tap + 1) * ch] = block.T.astype(BF16)


def columns_summed(acc, cols, ch):
    size = acc.shape[0]
    col = lax.broadcasted_iota(jnp.int32, (size, ch), 0) % cols
    left = jnp.where(col == 0, 0.0, pltpu.roll(acc[:, :ch], 1, 0))
    right = jnp.where(col == cols - 1, 0.0, pltpu.roll(acc[:, 2 * ch :], size - 1, 0))
    return left + acc[:, ch : 2 * ch] + right


def taps(windows, weight):
    ch = weight.shape[-1]
    lhs = jnp.concatenate(windows, axis=1)
    rhs = jnp.concatenate([weight[:, kw].reshape(3 * ch, ch) for kw in range(3)], axis=1)
    return jnp.dot(lhs, rhs, preferred_element_type=F32)


def inner_kernel(flags, prev, gain, res_held, partial, out, act):
    rows, cols, ch = act.shape[1:]
    keep = flags[0].astype(F32)
    act[...] = (activated(prev[...].astype(F32), gain[...].reshape(1, 1, 1, ch)) * keep).astype(BF16)
    both = taps(inner_windows(act, 0, 2, cols, ch), res_held.at[0])
    early = taps(inner_windows(act, 1, 1, cols, ch), res_held.at[1])
    half = early.shape[0]
    acc = jnp.concatenate([both[:half] + early, both[half:]], axis=0)
    branch = columns_summed(acc, cols, ch).reshape(2, rows - 2, cols, ch)
    out[...] = (partial[...] + branch).astype(BF16)


def halo_kernel(flags, cross, pair, gain, out):
    ch = pair.shape[-1]
    odd = flags[3]
    inside = jnp.where(odd == 1, flags[2], flags[1]).astype(F32)
    g = gain[...].reshape(1, 1, 1, ch)
    out[:, 1 - odd] = activated(pair[...].astype(F32), g).astype(BF16)
    out[:, odd] = (activated(cross[...].astype(F32), g) * inside).astype(BF16)


def rim_windows(act, start, count, cols, ch):
    return [
        act[start : start + count, :, kh : kh + 2].reshape(count * 4 * cols, ch) for kh in range(3)
    ]


def rim_own_kernel(flags, act_own, halo, own, cross, pair, res_held, out, act):
    rows, cols, ch = own.shape[1:]
    odd = flags[3]
    act[:, 0, 0:2] = halo[:, 0]
    act[:, 0, 2:4] = act_own[:, 0:2]
    act[:, 1, 0:2] = act_own[:, rows - 2 : rows]
    act[:, 1, 2:4] = halo[:, 1]
    both = taps(rim_windows(act, 0, 2, cols, ch), res_held.at[2])
    late = taps(rim_windows(act, 0, 1, cols, ch), res_held.at[1])
    half = late.shape[0]
    acc = jnp.concatenate([both[:half], both[half:] + late], axis=0)
    branch = columns_summed(acc, cols, ch).reshape(2, 2, 2, cols, ch)
    out[:, 0, 1] = own[:, 0].astype(F32) + branch[:, 0, 1]
    out[:, 1, 0] = own[:, rows - 1].astype(F32) + branch[:, 1, 0]
    above = jnp.where(odd == 1, pair[:, 1].astype(F32), cross[:, 1].astype(F32))
    below = jnp.where(odd == 1, cross[:, 0].astype(F32), pair[:, 0].astype(F32))
    out[:, 0, 0] = above + branch[:, 0, 0]
    out[:, 1, 1] = below + branch[:, 1, 1]


def rim_value(flags, act_prev, halo, partial, res_held, out, act):
    rows = act_prev.shape[1]
    cols, ch = partial.shape[3:]
    keep = flags[0].astype(BF16)
    act[:, 0, 0:2] = halo[:, 0] * keep
    act[:, 0, 2:4] = act_prev[:, 0:2]
    act[:, 1, 0:2] = act_prev[:, rows - 2 : rows]
    act[:, 1, 2:4] = halo[:, 1] * keep
    both = taps(rim_windows(act, 0, 2, cols, ch), res_held.at[0])
    early = taps(rim_windows(act, 1, 1, cols, ch), res_held.at[1])
    half = early.shape[0]
    acc = jnp.concatenate([both[:half] + early, both[half:]], axis=0)
    blended = partial[...] + columns_summed(acc, cols, ch).reshape(2, 2, 2, cols, ch)
    out[:, 0, 0] = (blended[:, 0, 0] * flags[1].astype(F32)).astype(BF16)
    out[:, 0, 1] = blended[:, 0, 1].astype(BF16)
    out[:, 1, 0] = blended[:, 1, 0].astype(BF16)
    out[:, 1, 1] = (blended[:, 1, 1] * flags[2].astype(F32)).astype(BF16)


def rim_first_kernel(flags, act_prev, halo, partial, res_held, up_weight, out, combined, act):
    @pl.when(flags[4] == 1)
    def _():
        rim_value(flags, act_prev, halo, partial, res_held, out, act)

    @pl.when(flags[4] == 0)
    def _():
        out[...] = jnp.zeros(out.shape, BF16)
        combine(up_weight, combined)


def rim_second_kernel(flags, act_prev, halo, partial, res_held, up_weight, out, combined, act):
    @pl.when(flags[4] == 0)
    def _():
        rim_value(flags, act_prev, halo, partial, res_held, out, act)

    @pl.when(flags[4] == 1)
    def _():
        out[...] = jnp.zeros(out.shape, BF16)
        combine(up_weight, combined)


def time_products(windows, weight, first):
    ch = weight.shape[1]
    count = len(windows)
    lhs = jnp.concatenate(windows, axis=1) if count > 1 else windows[0]
    rhs = weight[first : first + count].reshape(count * ch, 2 * ch)
    return jnp.dot(lhs, rhs, preferred_element_type=F32)


def woven_columns(upper, lower, weight, woven, cols, co):
    y = jnp.dot(jnp.concatenate([upper, lower], axis=1), weight, preferred_element_type=F32)
    size = y.shape[0]
    a, b = y[:, : 2 * co], y[:, 2 * co :]
    col = lax.broadcasted_iota(jnp.int32, (size, 2 * co), 0) % cols
    lane = lax.broadcasted_iota(jnp.int32, (size, 2 * co), 1)
    shift_a = jnp.where(col == 0, 0.0, pltpu.roll(a, 1, 0))
    shift_b = jnp.where(col == cols - 1, 0.0, pltpu.roll(b, size - 1, 0))
    z = jnp.where(lane < co, shift_a + b, a + shift_b)
    for parity, value in ((0, z), (1, pltpu.roll(z, co, 1))):
        for half in range(2):
            woven[half, pl.ds(parity, size, 2), :] = value[:, half * 128 : half * 128 + 128]

    def line(index):
        at = index * 2 * cols
        both = jnp.concatenate([woven[half, at : at + 2 * cols] for half in range(2)], axis=1)
        return both[:, :co].astype(BF16)

    return line


def by_core(kernel, flags, *refs):
    second, first, *rest = refs

    @pl.when(flags[4] == 0)
    def _():
        kernel(flags, first, *rest)

    @pl.when(flags[4] == 1)
    def _():
        kernel(flags, second, *rest)


def up_inner_kernel(
    flags, weight, own, prev, rim_first, rim_second, time_weight, stage, inner_rim, rim_part, stack, up, woven
):
    frames, lines, cols, ch = own.shape
    co = stage.shape[-1]
    stack[2:4] = own[...]
    stack[0:2] = prev[...] * flags[0].astype(BF16)
    size = frames * lines * cols
    windows = [stack[k : k + 2].reshape(size, ch) for k in range(3)]
    doubled = time_products(windows, time_weight, 0).astype(BF16).reshape(frames, lines, cols, 2 * ch)
    for p in range(2):
        up[:, p] = doubled[..., p * ch : (p + 1) * ch]
    for p in range(2):
        inner_rim[:, p, 0] = up[:, p, 0]
        inner_rim[:, p, 1] = up[:, p, lines - 1]
    pairs = lines - 1
    size = 2 * frames * pairs * cols
    upper = up[:, :, 0:pairs].reshape(size, ch)
    lower = up[:, :, 1 : pairs + 1].reshape(size, ch)
    for phase in range(2):
        line = woven_columns(upper, lower, weight[phase], woven, cols, co)
        for f in range(2 * frames):
            for j in range(pairs):
                stage[f, 2 * j + 1 - phase] = line(f * pairs + j)
    half = rim_first.shape[1] * rim_first.shape[2] * cols
    rim_own = jnp.where(flags[4] == 1, rim_first[...], rim_second[...])
    first = rim_own[0].reshape(half, ch)
    rim_part[0:half] = time_products([first], time_weight, 2)
    rim_part[half:] = time_products([first, rim_own[1].reshape(half, ch)], time_weight, 1)


def up_rim_kernel(
    flags, weight, part, second, first, inner_rim, inner_stage, time_weight, out, up, woven, stage, sems
):
    frames, sides, lines, cols, ch = first.shape
    co = out.shape[-1]
    middle = pltpu.make_async_copy(inner_stage, out.at[:, 3 : 3 + inner_stage.shape[1]], sems.at[6])
    middle.start()
    keep = flags[0].astype(BF16)
    half = sides * lines * cols
    prev = jnp.where(flags[4] == 1, second[...], first[...]) * keep
    before = prev[0].reshape(half, ch)
    last = prev[1].reshape(half, ch)
    products = (
        part[0:half] + time_products([before, last], time_weight, 0),
        part[half:] + time_products([last], time_weight, 0),
    )
    for frame in range(frames):
        doubled = products[frame].astype(BF16).reshape(sides * lines, cols, 2 * ch)
        for p in range(2):
            lot = doubled[..., p * ch : (p + 1) * ch]
            up[frame, p, 0, 0:2] = lot[0:2]
            up[frame, p, 1, 1:3] = lot[2:4]
            up[frame, p, 0, 2] = inner_rim[frame, p, 0]
            up[frame, p, 1, 0] = inner_rim[frame, p, 1]
    size = 2 * frames * 3 * cols
    start = out.shape[1] - 3
    copies = [middle]
    for phase in range(2):
        if phase == 0:
            picks = ((0, 0, 0), (0, 1, 2), (1, 0, start + 1))
        else:
            picks = ((0, 1, 1), (1, 0, start), (1, 1, start + 2))

        def taken(step):
            lines_taken = [up[:, :, s, i + step : i + step + 1] for s, i, _ in picks]
            return jnp.concatenate(lines_taken, axis=2).reshape(size, ch)

        line = woven_columns(taken(0), taken(1), weight[phase], woven, cols, co)
        for j, (_, _, row) in enumerate(picks):
            for f in range(2 * frames):
                stage[phase, j, f, 0] = line(f * 3 + j)
            copy = pltpu.make_async_copy(
                stage.at[phase, j], out.at[:, row : row + 1], sems.at[phase * 3 + j]
            )
            copy.start()
            copies.append(copy)
    for copy in copies:
        copy.wait()


def call(kernel, name, shapes, specs, scratch, mib, args, out_specs=None, in_out=None, us=1):
    several = isinstance(shapes, list)
    return pl.pallas_call(
        kernel,
        out_shape=shapes,
        in_specs=specs,
        out_specs=out_specs if out_specs is not None else ([VMEM] * len(shapes) if several else VMEM),
        scratch_shapes=scratch,
        compiler_params=pltpu.CompilerParams(vmem_limit_bytes=mib * 2**20),
        cost_estimate=pl.CostEstimate(flops=us * 10**9, bytes_accessed=us * 3 * 10**9 // 1000, transcendentals=0),
        input_output_aliases=in_out or {},
        name=name,
    )(*args)


def vmem_out(shape, dtype):
    return pltpu.VMEM(shape, dtype)


def in_hbm(array):
    return pltpu.with_memory_space_constraint(array, pltpu.HBM)


def in_vmem(array):
    return pltpu.with_memory_space_constraint(array, pltpu.VMEM)


def shards(features, norm_gain, res_weight, time_weight, up_weight):
    frames, rows, cols, ch = features.shape
    nt, nr = lax.axis_size("tm"), lax.axis_size("rows")
    co = up_weight.shape[-1]
    t, r = lax.axis_index("tm"), lax.axis_index("rows")
    flags = jnp.stack([t > 0, r > 0, r < nr - 1, (r & 1) == 1, (t & 1) == 1]).astype(jnp.int32)
    sizes = (nt, nr)
    shape = jax.ShapeDtypeStruct

    def paired(r):
        return r ^ 1

    def crossed(r):
        return min(max((r + 1 ^ 1) - 1, 0), nr - 1)

    def later(block):
        return moved(block, sizes, lambda t, r: ((t + 1) % nt, r))

    parity = call(parity_kernel, "parity", vmem_out((1, ch), F32), [SMEM], [], 1, (flags,), us=5)
    odd = parity.reshape(1, 1, 1, ch) > 0.5
    top, bottom = features[:, :2], features[:, -2:]
    to_pair = jnp.where(odd, top, bottom)
    to_cross = jnp.where(odd, bottom, top)
    to_cross, to_pair, sent = lax.optimization_barrier((to_cross, to_pair, features))
    prev = later(sent)
    cross = moved(to_cross, sizes, lambda t, r: (t, crossed(r)))
    pair = moved(to_pair, sizes, lambda t, r: (t, paired(r)))
    res_held = in_vmem(res_weight)
    up_turned = jnp.swapaxes(up_weight, 2, 3)
    own, act_own, gain, inner_own, up_held, time_held = call(
        prepare_kernel,
        "prepare",
        [
            vmem_out(features.shape, BF16),
            vmem_out(features.shape, BF16),
            vmem_out((1, ch), F32),
            vmem_out((2, rows - 2, cols, ch), F32),
            vmem_out(up_turned.shape, BF16),
            vmem_out(time_weight.shape, BF16),
        ],
        [HBM] * 4 + [VMEM],
        [pltpu.VMEM((ch,), F32), pltpu.SemaphoreType.DMA((4,))],
        16,
        (in_hbm(features), in_hbm(norm_gain), in_hbm(up_turned), in_hbm(time_weight), res_held),
        us=3,
    )
    lines = rows - 2
    halo = call(
        halo_kernel,
        "halo",
        vmem_out((2, 2, 2, cols, ch), BF16),
        [SMEM] + [VMEM] * 3,
        [],
        8,
        (flags, cross, pair, gain),
    )
    prev_halo = later(halo)
    act_prev_shape = vmem_out((2, rows, cols, ch), BF16)
    inner, act_prev = call(
        inner_kernel,
        "inner",
        [shape((2, lines, cols, ch), BF16), act_prev_shape],
        [SMEM] + [VMEM] * 4,
        [],
        16,
        (flags, prev, gain, res_held, inner_own),
    )
    inner_prev = later(inner)
    side_rows = [pltpu.VMEM((2, 2, 4, cols, ch), BF16)]
    rim_own = call(
        rim_own_kernel,
        "rim_own",
        vmem_out((2, 2, 2, cols, ch), F32),
        [SMEM] + [VMEM] * 6,
        side_rows,
        16,
        (flags, act_own, halo, own, cross, pair, res_held),
    )
    rim_shape = vmem_out((2, 2, 2, cols, ch), BF16)
    sums_shape = vmem_out((2, 2 * ch, 4 * co), BF16)
    first, first_sums = call(
        rim_first_kernel,
        "rim_first",
        [rim_shape, sums_shape],
        [SMEM] + [VMEM] * 5,
        side_rows,
        24,
        (flags, act_prev, prev_halo, rim_own, res_held, in_vmem(up_held)),
    )
    first_prev = later(first)
    rim, second_sums = call(
        rim_second_kernel,
        "rim_second",
        [rim_shape, sums_shape],
        [SMEM] + [VMEM] * 5,
        side_rows,
        24,
        (flags, act_prev, prev_halo, rim_own, res_held, in_vmem(up_held)),
    )
    second_prev = moved(rim, sizes, lambda t, r: (t ^ 1, r))
    stage, inner_rim, rim_part = call(
        functools.partial(by_core, up_inner_kernel),
        "up_inner",
        [
            vmem_out((2 * frames, 2 * (lines - 1), 2 * cols, co), BF16),
            vmem_out((2, 2, 2, cols, ch), BF16),
            vmem_out((frames * 4 * cols, 2 * ch), F32),
        ],
        [SMEM] + [VMEM] * 7,
        [
            pltpu.VMEM((4, lines, cols, ch), BF16),
            pltpu.VMEM((2, 2, lines, cols, ch), BF16),
            pltpu.VMEM((2, 2 * frames * (lines - 1) * 2 * cols, 128), F32),
        ],
        24,
        (flags, second_sums, first_sums, inner, inner_prev, first, rim, in_vmem(time_held)),
    )
    return call(
        functools.partial(by_core, up_rim_kernel),
        "up_rim",
        shape((2 * frames, 2 * rows, 2 * cols, co), BF16),
        [SMEM] + [VMEM] * 8,
        [
            pltpu.VMEM((2, 2, 2, 3, cols, ch), BF16),
            pltpu.VMEM((2, 2 * frames * 3 * 2 * cols, 128), F32),
            pltpu.VMEM((2, 3, 2 * frames, 1, 2 * cols, co), BF16),
            pltpu.SemaphoreType.DMA((7,)),
        ],
        24,
        (flags, second_sums, first_sums, rim_part, second_prev, first_prev, inner_rim, stage, in_vmem(time_held)),
        out_specs=HBM,
    )


def solution(mesh):
    placed = (P("tm", "rows", None, None), P(), P(), P(), P())
    return jax.shard_map(
        shards, mesh=mesh, in_specs=placed, out_specs=P("tm", "rows", None, None), check_vma=False
    )
```

```python
import jax
import jax.numpy as jnp
from jax import lax
from jax.experimental import pallas as pl
from jax.experimental.pallas import tpu as pltpu
from jax.sharding import PartitionSpec as P

F32 = jnp.float32
BF16 = jnp.bfloat16
VMEM = pl.BlockSpec(memory_space=pltpu.VMEM)
HBM = pl.BlockSpec(memory_space=pltpu.HBM)


def moved(block, sizes, target):
    nt, nr = sizes
    pairs = []
    for t in range(nt):
        for r in range(nr):
            to_t, to_r = target(t, r)
            pairs.append((t * nr + r, to_t * nr + to_r))
    return lax.ppermute(block, ("tm", "rows"), pairs)


def place():
    t, r = lax.axis_index("tm"), lax.axis_index("rows")
    conditions = (t > 0, r > 0, r < lax.axis_size("rows") - 1, (r & 1) == 1)
    return [condition.astype(jnp.int32) for condition in conditions]


def activated(values, gain):
    inv = lax.rsqrt(jnp.mean(values * values, axis=-1, keepdims=True) + 1e-06)
    half = values * inv * gain * 0.5
    return half + half * jnp.tanh(half)


def inner_windows(act, start, count, cols, ch):
    lines = act.shape[1] - 2
    return [
        act[start : start + count, kh : kh + lines].reshape(count * lines * cols, ch)
        for kh in range(3)
    ]


def prepare_kernel(
    features, gain, res_weight, own, act, gain_out, res_held, partial, gain_in, sems
):
    rows, cols, ch = own.shape[1:]
    copies = [
        pltpu.make_async_copy(source, target, sems.at[i])
        for i, (source, target) in enumerate(
            ((gain, gain_in), (features, own))
            + tuple((res_weight.at[kt], res_held.at[kt]) for kt in (2, 1, 0))
        )
    ]
    for copy in copies:
        copy.start()
    copies[0].wait()
    copies[1].wait()
    g = gain_in[...].reshape(1, ch)
    gain_out[...] = g
    act[...] = activated(own[...].astype(F32), g.reshape(1, 1, 1, ch)).astype(BF16)
    copies[2].wait()
    both = taps(inner_windows(act, 0, 2, cols, ch), res_held.at[2])
    copies[3].wait()
    late = taps(inner_windows(act, 0, 1, cols, ch), res_held.at[1])
    half = late.shape[0]
    acc = jnp.concatenate([both[:half], both[half:] + late], axis=0)
    branch = columns_summed(acc, cols, ch).reshape(2, rows - 2, cols, ch)
    partial[...] = own[:, 1 : rows - 1].astype(F32) + branch
    copies[4].wait()


def combine_kernel(up_weight, time_weight, after, combined, time_out, up_in, sems):
    del after
    ch = time_out.shape[1]
    copies = [
        pltpu.make_async_copy(source, target, sems.at[i])
        for i, (source, target) in enumerate(((up_weight, up_in), (time_weight, time_out)))
    ]
    for copy in copies:
        copy.start()
    copies[0].wait()
    w = [[up_in[kh, kw].astype(F32) for kw in range(3)] for kh in range(3)]
    for phase in range(2):
        for tap in range(2):
            if phase == 0:
                r = w[0] if tap == 0 else [w[1][k] + w[2][k] for k in range(3)]
            else:
                r = [w[0][k] + w[1][k] for k in range(3)] if tap == 0 else w[2]
            block = jnp.concatenate([r[0], r[0] + r[1], r[1] + r[2], r[2]], axis=0)
            combined[phase, tap * ch : (tap + 1) * ch] = block.T.astype(BF16)
    copies[1].wait()


def columns_summed(acc, cols, ch):
    size = acc.shape[0]
    col = lax.broadcasted_iota(jnp.int32, (size, ch), 0) % cols
    left = jnp.where(col == 0, 0.0, pltpu.roll(acc[:, :ch], 1, 0))
    right = jnp.where(col == cols - 1, 0.0, pltpu.roll(acc[:, 2 * ch :], size - 1, 0))
    return left + acc[:, ch : 2 * ch] + right


def taps(windows, weight):
    ch = weight.shape[-1]
    lhs = jnp.concatenate(windows, axis=1)
    rhs = jnp.concatenate([weight[:, kw].reshape(3 * ch, ch) for kw in range(3)], axis=1)
    return jnp.dot(lhs, rhs, preferred_element_type=F32)


def inner_kernel(prev, gain, res_held, partial, out, act):
    flags = place()
    rows, cols, ch = act.shape[1:]
    keep = flags[0].astype(F32)
    act[...] = (activated(prev[...].astype(F32), gain[...].reshape(1, 1, 1, ch)) * keep).astype(BF16)
    both = taps(inner_windows(act, 0, 2, cols, ch), res_held.at[0])
    early = taps(inner_windows(act, 1, 1, cols, ch), res_held.at[1])
    half = early.shape[0]
    acc = jnp.concatenate([both[:half] + early, both[half:]], axis=0)
    branch = columns_summed(acc, cols, ch).reshape(2, rows - 2, cols, ch)
    out[...] = (partial[...] + branch).astype(BF16)


def halo_kernel(cross, pair, gain, out):
    flags = place()
    ch = pair.shape[-1]
    odd = flags[3]
    inside = jnp.where(odd == 1, flags[2], flags[1]).astype(F32)
    g = gain[...].reshape(1, 1, 1, ch)
    out[:, 1 - odd] = activated(pair[...].astype(F32), g).astype(BF16)
    out[:, odd] = (activated(cross[...].astype(F32), g) * inside).astype(BF16)


def rim_windows(act, start, count, cols, ch):
    return [
        act[start : start + count, :, kh : kh + 2].reshape(count * 4 * cols, ch) for kh in range(3)
    ]


def rim_own_kernel(act_own, halo, own, cross, pair, res_held, out, act):
    flags = place()
    rows, cols, ch = own.shape[1:]
    odd = flags[3]
    act[:, 0, 0:2] = halo[:, 0]
    act[:, 0, 2:4] = act_own[:, 0:2]
    act[:, 1, 0:2] = act_own[:, rows - 2 : rows]
    act[:, 1, 2:4] = halo[:, 1]
    both = taps(rim_windows(act, 0, 2, cols, ch), res_held.at[2])
    late = taps(rim_windows(act, 0, 1, cols, ch), res_held.at[1])
    half = late.shape[0]
    acc = jnp.concatenate([both[:half], both[half:] + late], axis=0)
    branch = columns_summed(acc, cols, ch).reshape(2, 2, 2, cols, ch)
    out[:, 0, 1] = own[:, 0].astype(F32) + branch[:, 0, 1]
    out[:, 1, 0] = own[:, rows - 1].astype(F32) + branch[:, 1, 0]
    above = jnp.where(odd == 1, pair[:, 1].astype(F32), cross[:, 1].astype(F32))
    below = jnp.where(odd == 1, cross[:, 0].astype(F32), pair[:, 0].astype(F32))
    out[:, 0, 0] = above + branch[:, 0, 0]
    out[:, 1, 1] = below + branch[:, 1, 1]


def rim_kernel(act_prev, halo, partial, res_held, out, act):
    flags = place()
    rows = act_prev.shape[1]
    cols, ch = partial.shape[3:]
    keep = flags[0].astype(BF16)
    act[:, 0, 0:2] = halo[:, 0] * keep
    act[:, 0, 2:4] = act_prev[:, 0:2]
    act[:, 1, 0:2] = act_prev[:, rows - 2 : rows]
    act[:, 1, 2:4] = halo[:, 1] * keep
    both = taps(rim_windows(act, 0, 2, cols, ch), res_held.at[0])
    early = taps(rim_windows(act, 1, 1, cols, ch), res_held.at[1])
    half = early.shape[0]
    acc = jnp.concatenate([both[:half] + early, both[half:]], axis=0)
    blended = partial[...] + columns_summed(acc, cols, ch).reshape(2, 2, 2, cols, ch)
    out[:, 0, 0] = (blended[:, 0, 0] * flags[1].astype(F32)).astype(BF16)
    out[:, 0, 1] = blended[:, 0, 1].astype(BF16)
    out[:, 1, 0] = blended[:, 1, 0].astype(BF16)
    out[:, 1, 1] = (blended[:, 1, 1] * flags[2].astype(F32)).astype(BF16)


def time_products(windows, weight, first):
    ch = weight.shape[1]
    count = len(windows)
    lhs = jnp.concatenate(windows, axis=1) if count > 1 else windows[0]
    rhs = weight[first : first + count].reshape(count * ch, 2 * ch)
    return jnp.dot(lhs, rhs, preferred_element_type=F32)


def woven_columns(upper, lower, weight, woven, cols, co):
    y = jnp.dot(jnp.concatenate([upper, lower], axis=1), weight, preferred_element_type=F32)
    size = y.shape[0]
    a, b = y[:, : 2 * co], y[:, 2 * co :]
    col = lax.broadcasted_iota(jnp.int32, (size, 2 * co), 0) % cols
    lane = lax.broadcasted_iota(jnp.int32, (size, 2 * co), 1)
    shift_a = jnp.where(col == 0, 0.0, pltpu.roll(a, 1, 0))
    shift_b = jnp.where(col == cols - 1, 0.0, pltpu.roll(b, size - 1, 0))
    z = jnp.where(lane < co, shift_a + b, a + shift_b)
    for parity, value in ((0, z), (1, pltpu.roll(z, co, 1))):
        for half in range(2):
            woven[half, pl.ds(parity, size, 2), :] = value[:, half * 128 : half * 128 + 128]

    def line(index):
        at = index * 2 * cols
        both = jnp.concatenate([woven[half, at : at + 2 * cols] for half in range(2)], axis=1)
        return both[:, :co].astype(BF16)

    return line


def up_inner_kernel(own, prev, rim_own, time_weight, weight, stage, inner_rim, rim_part, stack, up, woven):
    flags = place()
    frames, lines, cols, ch = own.shape
    co = stage.shape[-1]
    stack[2:4] = own[...]
    stack[0:2] = prev[...] * flags[0].astype(BF16)
    size = frames * lines * cols
    windows = [stack[k : k + 2].reshape(size, ch) for k in range(3)]
    doubled = time_products(windows, time_weight, 0).astype(BF16).reshape(frames, lines, cols, 2 * ch)
    for p in range(2):
        up[:, p] = doubled[..., p * ch : (p + 1) * ch]
    for p in range(2):
        inner_rim[:, p, 0] = up[:, p, 0]
        inner_rim[:, p, 1] = up[:, p, lines - 1]
    pairs = lines - 1
    size = 2 * frames * pairs * cols
    upper = up[:, :, 0:pairs].reshape(size, ch)
    lower = up[:, :, 1 : pairs + 1].reshape(size, ch)
    for phase in range(2):
        line = woven_columns(upper, lower, weight[phase], woven, cols, co)
        for f in range(2 * frames):
            for j in range(pairs):
                stage[f, 2 * j + 1 - phase] = line(f * pairs + j)
    half = rim_own.shape[1] * rim_own.shape[2] * cols
    first = rim_own[0].reshape(half, ch)
    rim_part[0:half] = time_products([first], time_weight, 2)
    rim_part[half:] = time_products([first, rim_own[1].reshape(half, ch)], time_weight, 1)


def up_rim_kernel(
    part, prev, inner_rim, inner_stage, time_weight, weight, out, up, woven, stage, sems
):
    flags = place()
    frames, sides, lines, cols, ch = prev.shape
    co = out.shape[-1]
    middle = pltpu.make_async_copy(inner_stage, out.at[:, 3 : 3 + inner_stage.shape[1]], sems.at[6])
    middle.start()
    keep = flags[0].astype(BF16)
    half = sides * lines * cols
    before = prev[0].reshape(half, ch) * keep
    last = prev[1].reshape(half, ch) * keep
    products = (
        part[0:half] + time_products([before, last], time_weight, 0),
        part[half:] + time_products([last], time_weight, 0),
    )
    for frame in range(frames):
        doubled = products[frame].astype(BF16).reshape(sides * lines, cols, 2 * ch)
        for p in range(2):
            lot = doubled[..., p * ch : (p + 1) * ch]
            up[frame, p, 0, 0:2] = lot[0:2]
            up[frame, p, 1, 1:3] = lot[2:4]
            up[frame, p, 0, 2] = inner_rim[frame, p, 0]
            up[frame, p, 1, 0] = inner_rim[frame, p, 1]
    size = 2 * frames * 3 * cols
    start = out.shape[1] - 3
    copies = [middle]
    for phase in range(2):
        if phase == 0:
            picks = ((0, 0, 0), (0, 1, 2), (1, 0, start + 1))
        else:
            picks = ((0, 1, 1), (1, 0, start), (1, 1, start + 2))

        def taken(step):
            lines_taken = [up[:, :, s, i + step : i + step + 1] for s, i, _ in picks]
            return jnp.concatenate(lines_taken, axis=2).reshape(size, ch)

        line = woven_columns(taken(0), taken(1), weight[phase], woven, cols, co)
        for j, (_, _, row) in enumerate(picks):
            for f in range(2 * frames):
                stage[phase, j, f, 0] = line(f * 3 + j)
            copy = pltpu.make_async_copy(
                stage.at[phase, j], out.at[:, row : row + 1], sems.at[phase * 3 + j]
            )
            copy.start()
            copies.append(copy)
    for copy in copies:
        copy.wait()


def call(kernel, name, shapes, specs, scratch, mib, args, out_specs=None, us=1):
    several = isinstance(shapes, list)
    return pl.pallas_call(
        kernel,
        out_shape=shapes,
        in_specs=specs,
        out_specs=out_specs if out_specs is not None else ([VMEM] * len(shapes) if several else VMEM),
        scratch_shapes=scratch,
        compiler_params=pltpu.CompilerParams(vmem_limit_bytes=mib * 2**20),
        cost_estimate=pl.CostEstimate(flops=us * 10**9, bytes_accessed=us * 3 * 10**9 // 1000, transcendentals=0),
        name=name,
    )(*args)


def vmem_out(shape, dtype):
    return pltpu.VMEM(shape, dtype)


def in_hbm(array):
    return pltpu.with_memory_space_constraint(array, pltpu.HBM)


def in_vmem(array):
    return pltpu.with_memory_space_constraint(array, pltpu.VMEM)


def shards(features, norm_gain, res_weight, time_weight, up_weight):
    frames, rows, cols, ch = features.shape
    nt, nr = lax.axis_size("tm"), lax.axis_size("rows")
    co = up_weight.shape[-1]
    t, r = lax.axis_index("tm"), lax.axis_index("rows")
    sizes = (nt, nr)
    shape = jax.ShapeDtypeStruct

    def paired(r):
        return r ^ 1

    def crossed(r):
        return min(max((r + 1 ^ 1) - 1, 0), nr - 1)

    def later(block):
        return moved(block, sizes, lambda t, r: ((t + 1) % nt, r))

    odd = (r & 1) == 1
    top, bottom = features[:, :2], features[:, -2:]
    to_pair = jnp.where(odd, top, bottom)
    to_cross = jnp.where(odd, bottom, top)
    to_cross, to_pair, sent = lax.optimization_barrier((to_cross, to_pair, features))
    prev = later(sent)
    cross = moved(to_cross, sizes, lambda t, r: (t, crossed(r)))
    pair = moved(to_pair, sizes, lambda t, r: (t, paired(r)))
    own, act_own, gain, res_held, inner_own = call(
        prepare_kernel,
        "prepare",
        [
            vmem_out(features.shape, BF16),
            vmem_out(features.shape, BF16),
            vmem_out((1, ch), F32),
            vmem_out(res_weight.shape, BF16),
            vmem_out((2, rows - 2, cols, ch), F32),
        ],
        [HBM] * 3,
        [pltpu.VMEM((ch,), F32), pltpu.SemaphoreType.DMA((5,))],
        16,
        tuple(in_hbm(a) for a in (features, norm_gain, res_weight)),
    )
    lines = rows - 2
    halo = call(
        halo_kernel,
        "halo",
        vmem_out((2, 2, 2, cols, ch), BF16),
        [VMEM] * 3,
        [],
        8,
        (cross, pair, gain),
    )
    prev_halo = later(halo)
    act_prev_shape = vmem_out((2, rows, cols, ch), BF16)
    inner, act_prev = call(
        inner_kernel,
        "inner",
        [shape((2, lines, cols, ch), BF16), act_prev_shape],
        [VMEM] * 4,
        [],
        16,
        (prev, gain, in_vmem(res_held), inner_own),
    )
    inner_prev = later(inner)
    side_rows = [pltpu.VMEM((2, 2, 4, cols, ch), BF16)]
    rim_own = call(
        rim_own_kernel,
        "rim_own",
        vmem_out((2, 2, 2, cols, ch), F32),
        [VMEM] * 6,
        side_rows,
        16,
        (act_own, halo, own, cross, pair, in_vmem(res_held)),
    )
    rim = call(
        rim_kernel,
        "rim",
        shape((2, 2, 2, cols, ch), BF16),
        [VMEM] * 4,
        side_rows,
        16,
        (act_prev, prev_halo, rim_own, in_vmem(res_held)),
    )
    rim_prev = later(rim)
    up_turned = jnp.swapaxes(up_weight, 2, 3)
    combined, time_held = call(
        combine_kernel,
        "combine",
        [vmem_out((2, 2 * ch, 4 * co), BF16), vmem_out(time_weight.shape, BF16)],
        [HBM] * 2 + [VMEM],
        [pltpu.VMEM(up_turned.shape, BF16), pltpu.SemaphoreType.DMA((2,))],
        16,
        (in_hbm(up_turned), in_hbm(time_weight), rim),
    )
    stage, inner_rim, rim_part = call(
        up_inner_kernel,
        "up_inner",
        [
            vmem_out((2 * frames, 2 * (lines - 1), 2 * cols, co), BF16),
            vmem_out((2, 2, 2, cols, ch), BF16),
            vmem_out((frames * 4 * cols, 2 * ch), F32),
        ],
        [VMEM] * 5,
        [
            pltpu.VMEM((4, lines, cols, ch), BF16),
            pltpu.VMEM((2, 2, lines, cols, ch), BF16),
            pltpu.VMEM((2, 2 * frames * (lines - 1) * 2 * cols, 128), F32),
        ],
        24,
        (inner, inner_prev, rim, in_vmem(time_held), in_vmem(combined)),
    )
    return call(
        up_rim_kernel,
        "up_rim",
        shape((2 * frames, 2 * rows, 2 * cols, co), BF16),
        [VMEM] * 6,
        [
            pltpu.VMEM((2, 2, 2, 3, cols, ch), BF16),
            pltpu.VMEM((2, 2 * frames * 3 * 2 * cols, 128), F32),
            pltpu.VMEM((2, 3, 2 * frames, 1, 2 * cols, co), BF16),
            pltpu.SemaphoreType.DMA((7,)),
        ],
        24,
        (rim_part, rim_prev, inner_rim, stage, in_vmem(time_held), in_vmem(combined)),
        out_specs=HBM,
    )


def solution(mesh):
    placed = (P("tm", "rows", None, None), P(), P(), P(), P())
    return jax.shard_map(
        shards, mesh=mesh, in_specs=placed, out_specs=P("tm", "rows", None, None), check_vma=False
    )
```

```python
import functools

import jax
import jax.numpy as jnp
from jax import lax
from jax.experimental import pallas as pl
from jax.experimental.pallas import tpu as pltpu
from jax.sharding import PartitionSpec as P

F32 = jnp.float32
BF16 = jnp.bfloat16
VMEM = pl.BlockSpec(memory_space=pltpu.VMEM)
HBM = pl.BlockSpec(memory_space=pltpu.HBM)


def moved(block, sizes, target):
    nt, nr = sizes
    pairs = []
    for t in range(nt):
        for r in range(nr):
            to_t, to_r = target(t, r)
            pairs.append((t * nr + r, to_t * nr + to_r))
    return lax.ppermute(block, ("tm", "rows"), pairs)


def place():
    t, r = lax.axis_index("tm"), lax.axis_index("rows")
    conditions = (t > 0, r > 0, r < lax.axis_size("rows") - 1, (r & 1) == 1, (t & 1) == 1)
    return [condition.astype(jnp.int32) for condition in conditions]


def activated(values, gain):
    inv = lax.rsqrt(jnp.mean(values * values, axis=-1, keepdims=True) + 1e-06)
    half = values * inv * gain * 0.5
    return half + half * jnp.tanh(half)


def inner_windows(act, start, count, cols, ch):
    lines = act.shape[1] - 2
    return [
        act[start : start + count, kh : kh + lines].reshape(count * lines * cols, ch)
        for kh in range(3)
    ]


def parity_kernel(out):
    flags = place()
    out[...] = jnp.zeros(out.shape, F32) + flags[3].astype(F32)


def prepare_kernel(
    features, gain, up_weight, time_weight, res_held,
    own, act, gain_out, partial, up_out, time_out,
    gain_in, sems,
):
    rows, cols, ch = own.shape[1:]
    copies = [
        pltpu.make_async_copy(source, target, sems.at[i])
        for i, (source, target) in enumerate(
            ((gain, gain_in), (features, own), (up_weight, up_out), (time_weight, time_out))
        )
    ]
    for copy in copies:
        copy.start()
    copies[0].wait()
    copies[1].wait()
    g = gain_in[...].reshape(1, ch)
    gain_out[...] = g
    act[...] = activated(own[...].astype(F32), g.reshape(1, 1, 1, ch)).astype(BF16)
    both = taps(inner_windows(act, 0, 2, cols, ch), res_held.at[2])
    late = taps(inner_windows(act, 0, 1, cols, ch), res_held.at[1])
    half = late.shape[0]
    acc = jnp.concatenate([both[:half], both[half:] + late], axis=0)
    branch = columns_summed(acc, cols, ch).reshape(2, rows - 2, cols, ch)
    partial[...] = own[:, 1 : rows - 1].astype(F32) + branch
    copies[2].wait()
    copies[3].wait()


def combine(up_weight, combined):
    ch = up_weight.shape[-1]
    w = [[up_weight[kh, kw].astype(F32) for kw in range(3)] for kh in range(3)]
    for phase in range(2):
        for tap in range(2):
            if phase == 0:
                r = w[0] if tap == 0 else [w[1][k] + w[2][k] for k in range(3)]
            else:
                r = [w[0][k] + w[1][k] for k in range(3)] if tap == 0 else w[2]
            block = jnp.concatenate([r[0], r[0] + r[1], r[1] + r[2], r[2]], axis=0)
            combined[phase, tap * ch : (tap + 1) * ch] = block.T.astype(BF16)


def columns_summed(acc, cols, ch):
    size = acc.shape[0]
    col = lax.broadcasted_iota(jnp.int32, (size, ch), 0) % cols
    left = jnp.where(col == 0, 0.0, pltpu.roll(acc[:, :ch], 1, 0))
    right = jnp.where(col == cols - 1, 0.0, pltpu.roll(acc[:, 2 * ch :], size - 1, 0))
    return left + acc[:, ch : 2 * ch] + right


def taps(windows, weight):
    ch = weight.shape[-1]
    lhs = jnp.concatenate(windows, axis=1)
    rhs = jnp.concatenate([weight[:, kw].reshape(3 * ch, ch) for kw in range(3)], axis=1)
    return jnp.dot(lhs, rhs, preferred_element_type=F32)


def inner_kernel(prev, gain, res_held, partial, out, act):
    flags = place()
    rows, cols, ch = act.shape[1:]
    keep = flags[0].astype(F32)
    act[...] = (activated(prev[...].astype(F32), gain[...].reshape(1, 1, 1, ch)) * keep).astype(BF16)
    both = taps(inner_windows(act, 0, 2, cols, ch), res_held.at[0])
    early = taps(inner_windows(act, 1, 1, cols, ch), res_held.at[1])
    half = early.shape[0]
    acc = jnp.concatenate([both[:half] + early, both[half:]], axis=0)
    branch = columns_summed(acc, cols, ch).reshape(2, rows - 2, cols, ch)
    out[...] = (partial[...] + branch).astype(BF16)


def halo_kernel(cross, pair, gain, out):
    flags = place()
    ch = pair.shape[-1]
    odd = flags[3]
    inside = jnp.where(odd == 1, flags[2], flags[1]).astype(F32)
    g = gain[...].reshape(1, 1, 1, ch)
    out[:, 1 - odd] = activated(pair[...].astype(F32), g).astype(BF16)
    out[:, odd] = (activated(cross[...].astype(F32), g) * inside).astype(BF16)


def rim_windows(act, start, count, cols, ch):
    return [
        act[start : start + count, :, kh : kh + 2].reshape(count * 4 * cols, ch) for kh in range(3)
    ]


def rim_own_kernel(act_own, halo, own, cross, pair, res_held, out, act):
    flags = place()
    rows, cols, ch = own.shape[1:]
    odd = flags[3]
    act[:, 0, 0:2] = halo[:, 0]
    act[:, 0, 2:4] = act_own[:, 0:2]
    act[:, 1, 0:2] = act_own[:, rows - 2 : rows]
    act[:, 1, 2:4] = halo[:, 1]
    both = taps(rim_windows(act, 0, 2, cols, ch), res_held.at[2])
    late = taps(rim_windows(act, 0, 1, cols, ch), res_held.at[1])
    half = late.shape[0]
    acc = jnp.concatenate([both[:half], both[half:] + late], axis=0)
    branch = columns_summed(acc, cols, ch).reshape(2, 2, 2, cols, ch)
    out[:, 0, 1] = own[:, 0].astype(F32) + branch[:, 0, 1]
    out[:, 1, 0] = own[:, rows - 1].astype(F32) + branch[:, 1, 0]
    above = jnp.where(odd == 1, pair[:, 1].astype(F32), cross[:, 1].astype(F32))
    below = jnp.where(odd == 1, cross[:, 0].astype(F32), pair[:, 0].astype(F32))
    out[:, 0, 0] = above + branch[:, 0, 0]
    out[:, 1, 1] = below + branch[:, 1, 1]


def rim_value(flags, act_prev, halo, partial, res_held, out, act):
    rows = act_prev.shape[1]
    cols, ch = partial.shape[3:]
    keep = flags[0].astype(BF16)
    act[:, 0, 0:2] = halo[:, 0] * keep
    act[:, 0, 2:4] = act_prev[:, 0:2]
    act[:, 1, 0:2] = act_prev[:, rows - 2 : rows]
    act[:, 1, 2:4] = halo[:, 1] * keep
    both = taps(rim_windows(act, 0, 2, cols, ch), res_held.at[0])
    early = taps(rim_windows(act, 1, 1, cols, ch), res_held.at[1])
    half = early.shape[0]
    acc = jnp.concatenate([both[:half] + early, both[half:]], axis=0)
    blended = partial[...] + columns_summed(acc, cols, ch).reshape(2, 2, 2, cols, ch)
    out[:, 0, 0] = (blended[:, 0, 0] * flags[1].astype(F32)).astype(BF16)
    out[:, 0, 1] = blended[:, 0, 1].astype(BF16)
    out[:, 1, 0] = blended[:, 1, 0].astype(BF16)
    out[:, 1, 1] = (blended[:, 1, 1] * flags[2].astype(F32)).astype(BF16)


def rim_first_kernel(act_prev, halo, partial, res_held, up_weight, out, combined, act):
    flags = place()
    @pl.when(flags[4] == 1)
    def _():
        rim_value(flags, act_prev, halo, partial, res_held, out, act)

    @pl.when(flags[4] == 0)
    def _():
        out[...] = jnp.zeros(out.shape, BF16)
        combine(up_weight, combined)


def rim_second_kernel(act_prev, halo, partial, res_held, up_weight, out, combined, act):
    flags = place()
    @pl.when(flags[4] == 0)
    def _():
        rim_value(flags, act_prev, halo, partial, res_held, out, act)

    @pl.when(flags[4] == 1)
    def _():
        out[...] = jnp.zeros(out.shape, BF16)
        combine(up_weight, combined)


def time_products(windows, weight, first):
    ch = weight.shape[1]
    count = len(windows)
    lhs = jnp.concatenate(windows, axis=1) if count > 1 else windows[0]
    rhs = weight[first : first + count].reshape(count * ch, 2 * ch)
    return jnp.dot(lhs, rhs, preferred_element_type=F32)


def woven_columns(upper, lower, weight, woven, cols, co):
    y = jnp.dot(jnp.concatenate([upper, lower], axis=1), weight, preferred_element_type=F32)
    size = y.shape[0]
    a, b = y[:, : 2 * co], y[:, 2 * co :]
    col = lax.broadcasted_iota(jnp.int32, (size, 2 * co), 0) % cols
    lane = lax.broadcasted_iota(jnp.int32, (size, 2 * co), 1)
    shift_a = jnp.where(col == 0, 0.0, pltpu.roll(a, 1, 0))
    shift_b = jnp.where(col == cols - 1, 0.0, pltpu.roll(b, size - 1, 0))
    z = jnp.where(lane < co, shift_a + b, a + shift_b)
    for parity, value in ((0, z), (1, pltpu.roll(z, co, 1))):
        for half in range(2):
            woven[half, pl.ds(parity, size, 2), :] = value[:, half * 128 : half * 128 + 128]

    def line(index):
        at = index * 2 * cols
        both = jnp.concatenate([woven[half, at : at + 2 * cols] for half in range(2)], axis=1)
        return both[:, :co].astype(BF16)

    return line


def by_core(kernel, *refs):
    flags = place()
    second, first, *rest = refs

    @pl.when(flags[4] == 0)
    def _():
        kernel(flags, first, *rest)

    @pl.when(flags[4] == 1)
    def _():
        kernel(flags, second, *rest)


def up_inner_kernel(
    flags, weight, own, prev, rim_first, rim_second, time_weight, stage, inner_rim, rim_part, stack, up, woven
):
    frames, lines, cols, ch = own.shape
    co = stage.shape[-1]
    stack[2:4] = own[...]
    stack[0:2] = prev[...] * flags[0].astype(BF16)
    size = frames * lines * cols
    windows = [stack[k : k + 2].reshape(size, ch) for k in range(3)]
    doubled = time_products(windows, time_weight, 0).astype(BF16).reshape(frames, lines, cols, 2 * ch)
    for p in range(2):
        up[:, p] = doubled[..., p * ch : (p + 1) * ch]
    for p in range(2):
        inner_rim[:, p, 0] = up[:, p, 0]
        inner_rim[:, p, 1] = up[:, p, lines - 1]
    pairs = lines - 1
    size = 2 * frames * pairs * cols
    upper = up[:, :, 0:pairs].reshape(size, ch)
    lower = up[:, :, 1 : pairs + 1].reshape(size, ch)
    for phase in range(2):
        line = woven_columns(upper, lower, weight[phase], woven, cols, co)
        for f in range(2 * frames):
            for j in range(pairs):
                stage[f, 2 * j + 1 - phase] = line(f * pairs + j)
    half = rim_first.shape[1] * rim_first.shape[2] * cols
    rim_own = jnp.where(flags[4] == 1, rim_first[...], rim_second[...])
    first = rim_own[0].reshape(half, ch)
    rim_part[0:half] = time_products([first], time_weight, 2)
    rim_part[half:] = time_products([first, rim_own[1].reshape(half, ch)], time_weight, 1)


def up_rim_kernel(
    flags, weight, part, second, first, inner_rim, inner_stage, time_weight, out, up, woven, stage, sems
):
    frames, sides, lines, cols, ch = first.shape
    co = out.shape[-1]
    middle = pltpu.make_async_copy(inner_stage, out.at[:, 3 : 3 + inner_stage.shape[1]], sems.at[6])
    middle.start()
    keep = flags[0].astype(BF16)
    half = sides * lines * cols
    prev = jnp.where(flags[4] == 1, second[...], first[...]) * keep
    before = prev[0].reshape(half, ch)
    last = prev[1].reshape(half, ch)
    products = (
        part[0:half] + time_products([before, last], time_weight, 0),
        part[half:] + time_products([last], time_weight, 0),
    )
    for frame in range(frames):
        doubled = products[frame].astype(BF16).reshape(sides * lines, cols, 2 * ch)
        for p in range(2):
            lot = doubled[..., p * ch : (p + 1) * ch]
            up[frame, p, 0, 0:2] = lot[0:2]
            up[frame, p, 1, 1:3] = lot[2:4]
            up[frame, p, 0, 2] = inner_rim[frame, p, 0]
            up[frame, p, 1, 0] = inner_rim[frame, p, 1]
    size = 2 * frames * 3 * cols
    start = out.shape[1] - 3
    copies = [middle]
    for phase in range(2):
        if phase == 0:
            picks = ((0, 0, 0), (0, 1, 2), (1, 0, start + 1))
        else:
            picks = ((0, 1, 1), (1, 0, start), (1, 1, start + 2))

        def taken(step):
            lines_taken = [up[:, :, s, i + step : i + step + 1] for s, i, _ in picks]
            return jnp.concatenate(lines_taken, axis=2).reshape(size, ch)

        line = woven_columns(taken(0), taken(1), weight[phase], woven, cols, co)
        for j, (_, _, row) in enumerate(picks):
            for f in range(2 * frames):
                stage[phase, j, f, 0] = line(f * 3 + j)
            copy = pltpu.make_async_copy(
                stage.at[phase, j], out.at[:, row : row + 1], sems.at[phase * 3 + j]
            )
            copy.start()
            copies.append(copy)
    for copy in copies:
        copy.wait()


def call(kernel, name, shapes, specs, scratch, mib, args, out_specs=None, in_out=None, us=1):
    several = isinstance(shapes, list)
    return pl.pallas_call(
        kernel,
        out_shape=shapes,
        in_specs=specs,
        out_specs=out_specs if out_specs is not None else ([VMEM] * len(shapes) if several else VMEM),
        scratch_shapes=scratch,
        compiler_params=pltpu.CompilerParams(vmem_limit_bytes=mib * 2**20),
        cost_estimate=pl.CostEstimate(flops=us * 10**9, bytes_accessed=us * 3 * 10**9 // 1000, transcendentals=0),
        input_output_aliases=in_out or {},
        name=name,
    )(*args)


def vmem_out(shape, dtype):
    return pltpu.VMEM(shape, dtype)


def in_hbm(array):
    return pltpu.with_memory_space_constraint(array, pltpu.HBM)


def in_vmem(array):
    return pltpu.with_memory_space_constraint(array, pltpu.VMEM)


def shards(features, norm_gain, res_weight, time_weight, up_weight):
    frames, rows, cols, ch = features.shape
    nt, nr = lax.axis_size("tm"), lax.axis_size("rows")
    co = up_weight.shape[-1]
    t, r = lax.axis_index("tm"), lax.axis_index("rows")
    sizes = (nt, nr)
    shape = jax.ShapeDtypeStruct

    def paired(r):
        return r ^ 1

    def crossed(r):
        return min(max((r + 1 ^ 1) - 1, 0), nr - 1)

    def later(block):
        return moved(block, sizes, lambda t, r: ((t + 1) % nt, r))

    parity = call(parity_kernel, "parity", vmem_out((1, ch), F32), [], [], 1, (), us=5)
    odd = parity.reshape(1, 1, 1, ch) > 0.5
    top, bottom = features[:, :2], features[:, -2:]
    to_pair = jnp.where(odd, top, bottom)
    to_cross = jnp.where(odd, bottom, top)
    to_cross, to_pair, sent = lax.optimization_barrier((to_cross, to_pair, features))
    prev = later(sent)
    cross = moved(to_cross, sizes, lambda t, r: (t, crossed(r)))
    pair = moved(to_pair, sizes, lambda t, r: (t, paired(r)))
    res_held = in_vmem(res_weight)
    up_turned = jnp.swapaxes(up_weight, 2, 3)
    own, act_own, gain, inner_own, up_held, time_held = call(
        prepare_kernel,
        "prepare",
        [
            vmem_out(features.shape, BF16),
            vmem_out(features.shape, BF16),
            vmem_out((1, ch), F32),
            vmem_out((2, rows - 2, cols, ch), F32),
            vmem_out(up_turned.shape, BF16),
            vmem_out(time_weight.shape, BF16),
        ],
        [HBM] * 4 + [VMEM],
        [pltpu.VMEM((ch,), F32), pltpu.SemaphoreType.DMA((4,))],
        16,
        (in_hbm(features), in_hbm(norm_gain), in_hbm(up_turned), in_hbm(time_weight), res_held),
        us=3,
    )
    lines = rows - 2
    halo = call(
        halo_kernel,
        "halo",
        vmem_out((2, 2, 2, cols, ch), BF16),
        [VMEM] * 3,
        [],
        8,
        (cross, pair, gain),
    )
    prev_halo = later(halo)
    act_prev_shape = vmem_out((2, rows, cols, ch), BF16)
    inner, act_prev = call(
        inner_kernel,
        "inner",
        [shape((2, lines, cols, ch), BF16), act_prev_shape],
        [VMEM] * 4,
        [],
        16,
        (prev, gain, res_held, inner_own),
    )
    inner_prev = later(inner)
    side_rows = [pltpu.VMEM((2, 2, 4, cols, ch), BF16)]
    rim_own = call(
        rim_own_kernel,
        "rim_own",
        vmem_out((2, 2, 2, cols, ch), F32),
        [VMEM] * 6,
        side_rows,
        16,
        (act_own, halo, own, cross, pair, res_held),
    )
    rim_shape = vmem_out((2, 2, 2, cols, ch), BF16)
    sums_shape = vmem_out((2, 2 * ch, 4 * co), BF16)
    first, first_sums = call(
        rim_first_kernel,
        "rim_first",
        [rim_shape, sums_shape],
        [VMEM] * 5,
        side_rows,
        24,
        (act_prev, prev_halo, rim_own, res_held, in_vmem(up_held)),
    )
    first_prev = later(first)
    rim, second_sums = call(
        rim_second_kernel,
        "rim_second",
        [rim_shape, sums_shape],
        [VMEM] * 5,
        side_rows,
        24,
        (act_prev, prev_halo, rim_own, res_held, in_vmem(up_held)),
    )
    second_prev = moved(rim, sizes, lambda t, r: (t ^ 1, r))
    stage, inner_rim, rim_part = call(
        functools.partial(by_core, up_inner_kernel),
        "up_inner",
        [
            vmem_out((2 * frames, 2 * (lines - 1), 2 * cols, co), BF16),
            vmem_out((2, 2, 2, cols, ch), BF16),
            vmem_out((frames * 4 * cols, 2 * ch), F32),
        ],
        [VMEM] * 7,
        [
            pltpu.VMEM((4, lines, cols, ch), BF16),
            pltpu.VMEM((2, 2, lines, cols, ch), BF16),
            pltpu.VMEM((2, 2 * frames * (lines - 1) * 2 * cols, 128), F32),
        ],
        24,
        (second_sums, first_sums, inner, inner_prev, first, rim, in_vmem(time_held)),
    )
    return call(
        functools.partial(by_core, up_rim_kernel),
        "up_rim",
        shape((2 * frames, 2 * rows, 2 * cols, co), BF16),
        [VMEM] * 8,
        [
            pltpu.VMEM((2, 2, 2, 3, cols, ch), BF16),
            pltpu.VMEM((2, 2 * frames * 3 * 2 * cols, 128), F32),
            pltpu.VMEM((2, 3, 2 * frames, 1, 2 * cols, co), BF16),
            pltpu.SemaphoreType.DMA((7,)),
        ],
        24,
        (second_sums, first_sums, rim_part, second_prev, first_prev, inner_rim, stage, in_vmem(time_held)),
        out_specs=HBM,
    )


def solution(mesh):
    placed = (P("tm", "rows", None, None), P(), P(), P(), P())
    return jax.shard_map(
        shards, mesh=mesh, in_specs=placed, out_specs=P("tm", "rows", None, None), check_vma=False
    )
```

```python
import functools

import jax
import jax.numpy as jnp
from jax import lax
from jax.experimental import pallas as pl
from jax.experimental.pallas import tpu as pltpu
from jax.sharding import PartitionSpec as P

F32 = jnp.float32
BF16 = jnp.bfloat16
VMEM = pl.BlockSpec(memory_space=pltpu.VMEM)
HBM = pl.BlockSpec(memory_space=pltpu.HBM)


def moved(block, sizes, target):
    nt, nr = sizes
    pairs = []
    for t in range(nt):
        for r in range(nr):
            to_t, to_r = target(t, r)
            pairs.append((t * nr + r, to_t * nr + to_r))
    return lax.ppermute(block, ("tm", "rows"), pairs)


def place():
    t, r = lax.axis_index("tm"), lax.axis_index("rows")
    conditions = (t > 0, r > 0, r < lax.axis_size("rows") - 1, (r & 1) == 1, (t & 1) == 1)
    return [condition.astype(jnp.int32) for condition in conditions]


def activated(values, gain):
    inv = lax.rsqrt(jnp.mean(values * values, axis=-1, keepdims=True) + 1e-06)
    half = values * inv * gain * 0.5
    return half + half * jnp.tanh(half)


def inner_windows(act, start, count, cols, ch):
    lines = act.shape[1] - 2
    return [
        act[start : start + count, kh : kh + lines].reshape(count * lines * cols, ch)
        for kh in range(3)
    ]


def parity_kernel(out):
    flags = place()
    out[...] = jnp.zeros(out.shape, F32) + flags[3].astype(F32)


def prepare_kernel(
    features, gain, up_weight, time_weight, res_held,
    own, act, gain_out, partial, up_out, time_out,
    gain_in, sems,
):
    rows, cols, ch = own.shape[1:]
    copies = [
        pltpu.make_async_copy(source, target, sems.at[i])
        for i, (source, target) in enumerate(
            ((gain, gain_in), (features, own), (up_weight, up_out), (time_weight, time_out))
        )
    ]
    for copy in copies:
        copy.start()
    copies[0].wait()
    copies[1].wait()
    g = gain_in[...].reshape(1, ch)
    gain_out[...] = g
    act[...] = activated(own[...].astype(F32), g.reshape(1, 1, 1, ch)).astype(BF16)
    both = taps(inner_windows(act, 0, 2, cols, ch), res_held.at[2])
    late = taps(inner_windows(act, 0, 1, cols, ch), res_held.at[1])
    half = late.shape[0]
    acc = jnp.concatenate([both[:half], both[half:] + late], axis=0)
    branch = columns_summed(acc, cols, ch).reshape(2, rows - 2, cols, ch)
    partial[...] = own[:, 1 : rows - 1].astype(F32) + branch
    copies[2].wait()
    copies[3].wait()


def combine(up_weight, combined):
    ch = up_weight.shape[-1]
    w = [[up_weight[kh, kw].astype(F32) for kw in range(3)] for kh in range(3)]
    for phase in range(2):
        for tap in range(2):
            if phase == 0:
                r = w[0] if tap == 0 else [w[1][k] + w[2][k] for k in range(3)]
            else:
                r = [w[0][k] + w[1][k] for k in range(3)] if tap == 0 else w[2]
            block = jnp.concatenate([r[0], r[0] + r[1], r[1] + r[2], r[2]], axis=0)
            combined[phase, tap * ch : (tap + 1) * ch] = block.astype(BF16).T


def columns_summed(acc, cols, ch):
    size = acc.shape[0]
    col = lax.broadcasted_iota(jnp.int32, (size, ch), 0) % cols
    left = jnp.where(col == 0, 0.0, pltpu.roll(acc[:, :ch], 1, 0))
    right = jnp.where(col == cols - 1, 0.0, pltpu.roll(acc[:, 2 * ch :], size - 1, 0))
    return left + acc[:, ch : 2 * ch] + right


def taps(windows, weight):
    ch = weight.shape[-1]
    lhs = jnp.concatenate(windows, axis=1)
    rhs = jnp.concatenate([weight[:, kw].reshape(3 * ch, ch) for kw in range(3)], axis=1)
    return jnp.dot(lhs, rhs, preferred_element_type=F32)


def inner_kernel(prev, gain, res_held, partial, out, act):
    flags = place()
    rows, cols, ch = act.shape[1:]
    keep = flags[0].astype(F32)
    act[...] = (activated(prev[...].astype(F32), gain[...].reshape(1, 1, 1, ch)) * keep).astype(BF16)
    both = taps(inner_windows(act, 0, 2, cols, ch), res_held.at[0])
    early = taps(inner_windows(act, 1, 1, cols, ch), res_held.at[1])
    half = early.shape[0]
    acc = jnp.concatenate([both[:half] + early, both[half:]], axis=0)
    branch = columns_summed(acc, cols, ch).reshape(2, rows - 2, cols, ch)
    out[...] = (partial[...] + branch).astype(BF16)


def halo_kernel(cross, pair, gain, out):
    flags = place()
    ch = pair.shape[-1]
    odd = flags[3]
    inside = jnp.where(odd == 1, flags[2], flags[1]).astype(F32)
    g = gain[...].reshape(1, 1, 1, ch)
    out[:, 1 - odd] = activated(pair[...].astype(F32), g).astype(BF16)
    out[:, odd] = (activated(cross[...].astype(F32), g) * inside).astype(BF16)


def rim_windows(act, start, count, cols, ch):
    return [
        act[start : start + count, :, kh : kh + 2].reshape(count * 4 * cols, ch) for kh in range(3)
    ]


def rim_own_kernel(act_own, halo, own, cross, pair, res_held, out, act):
    flags = place()
    rows, cols, ch = own.shape[1:]
    odd = flags[3]
    act[:, 0, 0:2] = halo[:, 0]
    act[:, 0, 2:4] = act_own[:, 0:2]
    act[:, 1, 0:2] = act_own[:, rows - 2 : rows]
    act[:, 1, 2:4] = halo[:, 1]
    both = taps(rim_windows(act, 0, 2, cols, ch), res_held.at[2])
    late = taps(rim_windows(act, 0, 1, cols, ch), res_held.at[1])
    half = late.shape[0]
    acc = jnp.concatenate([both[:half], both[half:] + late], axis=0)
    branch = columns_summed(acc, cols, ch).reshape(2, 2, 2, cols, ch)
    out[:, 0, 1] = own[:, 0].astype(F32) + branch[:, 0, 1]
    out[:, 1, 0] = own[:, rows - 1].astype(F32) + branch[:, 1, 0]
    above = jnp.where(odd == 1, pair[:, 1].astype(F32), cross[:, 1].astype(F32))
    below = jnp.where(odd == 1, cross[:, 0].astype(F32), pair[:, 0].astype(F32))
    out[:, 0, 0] = above + branch[:, 0, 0]
    out[:, 1, 1] = below + branch[:, 1, 1]


def rim_value(flags, act_prev, halo, partial, res_held, out, act):
    rows = act_prev.shape[1]
    cols, ch = partial.shape[3:]
    keep = flags[0].astype(BF16)
    act[:, 0, 0:2] = halo[:, 0] * keep
    act[:, 0, 2:4] = act_prev[:, 0:2]
    act[:, 1, 0:2] = act_prev[:, rows - 2 : rows]
    act[:, 1, 2:4] = halo[:, 1] * keep
    both = taps(rim_windows(act, 0, 2, cols, ch), res_held.at[0])
    early = taps(rim_windows(act, 1, 1, cols, ch), res_held.at[1])
    half = early.shape[0]
    acc = jnp.concatenate([both[:half] + early, both[half:]], axis=0)
    blended = partial[...] + columns_summed(acc, cols, ch).reshape(2, 2, 2, cols, ch)
    out[:, 0, 0] = (blended[:, 0, 0] * flags[1].astype(F32)).astype(BF16)
    out[:, 0, 1] = blended[:, 0, 1].astype(BF16)
    out[:, 1, 0] = blended[:, 1, 0].astype(BF16)
    out[:, 1, 1] = (blended[:, 1, 1] * flags[2].astype(F32)).astype(BF16)


def rim_first_kernel(act_prev, halo, partial, res_held, up_weight, out, combined, act):
    flags = place()
    @pl.when(flags[4] == 1)
    def _():
        rim_value(flags, act_prev, halo, partial, res_held, out, act)

    @pl.when(flags[4] == 0)
    def _():
        out[...] = jnp.zeros(out.shape, BF16)
        combine(up_weight, combined)


def rim_second_kernel(act_prev, halo, partial, res_held, up_weight, out, combined, act):
    flags = place()
    @pl.when(flags[4] == 0)
    def _():
        rim_value(flags, act_prev, halo, partial, res_held, out, act)

    @pl.when(flags[4] == 1)
    def _():
        out[...] = jnp.zeros(out.shape, BF16)
        combine(up_weight, combined)


def time_products(windows, weight, first):
    ch = weight.shape[1]
    count = len(windows)
    lhs = jnp.concatenate(windows, axis=1) if count > 1 else windows[0]
    rhs = weight[first : first + count].reshape(count * ch, 2 * ch)
    return jnp.dot(lhs, rhs, preferred_element_type=F32)


def both_lines(upper, lower, weight):
    return jnp.dot(jnp.concatenate([upper, lower], axis=1), weight, preferred_element_type=F32)


def woven_columns(y, woven, cols, co):
    size = y.shape[0]
    a, b = y[:, : 2 * co], y[:, 2 * co :]
    col = lax.broadcasted_iota(jnp.int32, (size, 2 * co), 0) % cols
    lane = lax.broadcasted_iota(jnp.int32, (size, 2 * co), 1)
    shift_a = jnp.where(col == 0, 0.0, pltpu.roll(a, 1, 0))
    shift_b = jnp.where(col == cols - 1, 0.0, pltpu.roll(b, size - 1, 0))
    z = jnp.where(lane < co, shift_a + b, a + shift_b)
    for parity, value in ((0, z), (1, pltpu.roll(z, co, 1))):
        for half in range(2):
            woven[half, pl.ds(parity, size, 2), :] = value[:, half * 128 : half * 128 + 128]

    def line(index):
        at = index * 2 * cols
        both = jnp.concatenate([woven[half, at : at + 2 * cols] for half in range(2)], axis=1)
        return both[:, :co].astype(BF16)

    return line


def by_core(kernel, *refs):
    flags = place()
    second, first, *rest = refs

    @pl.when(flags[4] == 0)
    def _():
        kernel(flags, first, *rest)

    @pl.when(flags[4] == 1)
    def _():
        kernel(flags, second, *rest)


def up_inner_kernel(
    flags, weight, own, prev, rim_first, rim_second, time_weight, stage, inner_rim, rim_part, stack, up, woven
):
    frames, lines, cols, ch = own.shape
    co = stage.shape[-1]
    stack[2:4] = own[...]
    stack[0:2] = prev[...] * flags[0].astype(BF16)
    size = frames * lines * cols
    windows = [stack[k : k + 2].reshape(size, ch) for k in range(3)]
    doubled = time_products(windows, time_weight, 0).astype(BF16).reshape(frames, lines, cols, 2 * ch)
    for p in range(2):
        up[:, p] = doubled[..., p * ch : (p + 1) * ch]
    for p in range(2):
        inner_rim[:, p, 0] = up[:, p, 0]
        inner_rim[:, p, 1] = up[:, p, lines - 1]
    pairs = lines - 1
    size = 2 * frames * pairs * cols
    upper = up[:, :, 0:pairs].reshape(size, ch)
    lower = up[:, :, 1 : pairs + 1].reshape(size, ch)
    wide = both_lines(upper, lower, jnp.concatenate([weight[0], weight[1]], axis=1))
    for phase in range(2):
        line = woven_columns(wide[:, phase * 4 * co : (phase + 1) * 4 * co], woven, cols, co)
        for f in range(2 * frames):
            for j in range(pairs):
                stage[f, 2 * j + 1 - phase] = line(f * pairs + j)
    half = rim_first.shape[1] * rim_first.shape[2] * cols
    rim_own = jnp.where(flags[4] == 1, rim_first[...], rim_second[...])
    first = rim_own[0].reshape(half, ch)
    rim_part[0:half] = time_products([first], time_weight, 2)
    rim_part[half:] = time_products([first, rim_own[1].reshape(half, ch)], time_weight, 1)


def up_rim_kernel(
    flags, weight, part, second, first, inner_rim, inner_stage, time_weight, out, up, woven, stage, sems
):
    frames, sides, lines, cols, ch = first.shape
    co = out.shape[-1]
    middle = pltpu.make_async_copy(inner_stage, out.at[:, 3 : 3 + inner_stage.shape[1]], sems.at[6])
    middle.start()
    keep = flags[0].astype(BF16)
    half = sides * lines * cols
    prev = jnp.where(flags[4] == 1, second[...], first[...]) * keep
    before = prev[0].reshape(half, ch)
    last = prev[1].reshape(half, ch)
    products = (
        part[0:half] + time_products([before, last], time_weight, 0),
        part[half:] + time_products([last], time_weight, 0),
    )
    for frame in range(frames):
        doubled = products[frame].astype(BF16).reshape(sides * lines, cols, 2 * ch)
        for p in range(2):
            lot = doubled[..., p * ch : (p + 1) * ch]
            up[frame, p, 0, 0:2] = lot[0:2]
            up[frame, p, 1, 1:3] = lot[2:4]
            up[frame, p, 0, 2] = inner_rim[frame, p, 0]
            up[frame, p, 1, 0] = inner_rim[frame, p, 1]
    size = 2 * frames * 3 * cols
    start = out.shape[1] - 3
    copies = [middle]
    for phase in range(2):
        if phase == 0:
            picks = ((0, 0, 0), (0, 1, 2), (1, 0, start + 1))
        else:
            picks = ((0, 1, 1), (1, 0, start), (1, 1, start + 2))

        def taken(step):
            lines_taken = [up[:, :, s, i + step : i + step + 1] for s, i, _ in picks]
            return jnp.concatenate(lines_taken, axis=2).reshape(size, ch)

        line = woven_columns(both_lines(taken(0), taken(1), weight[phase]), woven, cols, co)
        for j, (_, _, row) in enumerate(picks):
            for f in range(2 * frames):
                stage[phase, j, f, 0] = line(f * 3 + j)
            copy = pltpu.make_async_copy(
                stage.at[phase, j], out.at[:, row : row + 1], sems.at[phase * 3 + j]
            )
            copy.start()
            copies.append(copy)
    for copy in copies:
        copy.wait()


def call(kernel, name, shapes, specs, scratch, mib, args, out_specs=None, in_out=None, us=1):
    several = isinstance(shapes, list)
    return pl.pallas_call(
        kernel,
        out_shape=shapes,
        in_specs=specs,
        out_specs=out_specs if out_specs is not None else ([VMEM] * len(shapes) if several else VMEM),
        scratch_shapes=scratch,
        compiler_params=pltpu.CompilerParams(vmem_limit_bytes=mib * 2**20),
        cost_estimate=pl.CostEstimate(flops=us * 10**9, bytes_accessed=us * 3 * 10**9 // 1000, transcendentals=0),
        input_output_aliases=in_out or {},
        name=name,
    )(*args)


def vmem_out(shape, dtype):
    return pltpu.VMEM(shape, dtype)


def in_hbm(array):
    return pltpu.with_memory_space_constraint(array, pltpu.HBM)


def in_vmem(array):
    return pltpu.with_memory_space_constraint(array, pltpu.VMEM)


def shards(features, norm_gain, res_weight, time_weight, up_weight):
    frames, rows, cols, ch = features.shape
    nt, nr = lax.axis_size("tm"), lax.axis_size("rows")
    co = up_weight.shape[-1]
    t, r = lax.axis_index("tm"), lax.axis_index("rows")
    sizes = (nt, nr)
    shape = jax.ShapeDtypeStruct

    def paired(r):
        return r ^ 1

    def crossed(r):
        return min(max((r + 1 ^ 1) - 1, 0), nr - 1)

    def later(block):
        return moved(block, sizes, lambda t, r: ((t + 1) % nt, r))

    parity = call(parity_kernel, "parity", vmem_out((1, ch), F32), [], [], 1, (), us=5)
    odd = parity.reshape(1, 1, 1, ch) > 0.5
    top, bottom = features[:, :2], features[:, -2:]
    to_pair = jnp.where(odd, top, bottom)
    to_cross = jnp.where(odd, bottom, top)
    to_cross, to_pair, sent = lax.optimization_barrier((to_cross, to_pair, features))
    prev = later(sent)
    cross = moved(to_cross, sizes, lambda t, r: (t, crossed(r)))
    pair = moved(to_pair, sizes, lambda t, r: (t, paired(r)))
    res_held = in_vmem(res_weight)
    up_turned = jnp.swapaxes(up_weight, 2, 3)
    own, act_own, gain, inner_own, up_held, time_held = call(
        prepare_kernel,
        "prepare",
        [
            vmem_out(features.shape, BF16),
            vmem_out(features.shape, BF16),
            vmem_out((1, ch), F32),
            vmem_out((2, rows - 2, cols, ch), F32),
            vmem_out(up_turned.shape, BF16),
            vmem_out(time_weight.shape, BF16),
        ],
        [HBM] * 4 + [VMEM],
        [pltpu.VMEM((ch,), F32), pltpu.SemaphoreType.DMA((4,))],
        16,
        (in_hbm(features), in_hbm(norm_gain), in_hbm(up_turned), in_hbm(time_weight), res_held),
        us=3,
    )
    lines = rows - 2
    halo = call(
        halo_kernel,
        "halo",
        vmem_out((2, 2, 2, cols, ch), BF16),
        [VMEM] * 3,
        [],
        8,
        (cross, pair, gain),
    )
    prev_halo = later(halo)
    act_prev_shape = vmem_out((2, rows, cols, ch), BF16)
    inner, act_prev = call(
        inner_kernel,
        "inner",
        [shape((2, lines, cols, ch), BF16), act_prev_shape],
        [VMEM] * 4,
        [],
        16,
        (prev, gain, res_held, inner_own),
    )
    inner_prev = later(inner)
    side_rows = [pltpu.VMEM((2, 2, 4, cols, ch), BF16)]
    rim_own = call(
        rim_own_kernel,
        "rim_own",
        vmem_out((2, 2, 2, cols, ch), F32),
        [VMEM] * 6,
        side_rows,
        16,
        (act_own, halo, own, cross, pair, res_held),
    )
    rim_shape = vmem_out((2, 2, 2, cols, ch), BF16)
    sums_shape = vmem_out((2, 2 * ch, 4 * co), BF16)
    first, first_sums = call(
        rim_first_kernel,
        "rim_first",
        [rim_shape, sums_shape],
        [VMEM] * 5,
        side_rows,
        24,
        (act_prev, prev_halo, rim_own, res_held, in_vmem(up_held)),
    )
    first_prev = later(first)
    rim, second_sums = call(
        rim_second_kernel,
        "rim_second",
        [rim_shape, sums_shape],
        [VMEM] * 5,
        side_rows,
        24,
        (act_prev, prev_halo, rim_own, res_held, in_vmem(up_held)),
    )
    second_prev = moved(rim, sizes, lambda t, r: (t ^ 1, r))
    stage, inner_rim, rim_part = call(
        functools.partial(by_core, up_inner_kernel),
        "up_inner",
        [
            vmem_out((2 * frames, 2 * (lines - 1), 2 * cols, co), BF16),
            vmem_out((2, 2, 2, cols, ch), BF16),
            vmem_out((frames * 4 * cols, 2 * ch), F32),
        ],
        [VMEM] * 7,
        [
            pltpu.VMEM((4, lines, cols, ch), BF16),
            pltpu.VMEM((2, 2, lines, cols, ch), BF16),
            pltpu.VMEM((2, 2 * frames * (lines - 1) * 2 * cols, 128), F32),
        ],
        24,
        (second_sums, first_sums, inner, inner_prev, first, rim, in_vmem(time_held)),
    )
    return call(
        functools.partial(by_core, up_rim_kernel),
        "up_rim",
        shape((2 * frames, 2 * rows, 2 * cols, co), BF16),
        [VMEM] * 8,
        [
            pltpu.VMEM((2, 2, 2, 3, cols, ch), BF16),
            pltpu.VMEM((2, 2 * frames * 3 * 2 * cols, 128), F32),
            pltpu.VMEM((2, 3, 2 * frames, 1, 2 * cols, co), BF16),
            pltpu.SemaphoreType.DMA((7,)),
        ],
        24,
        (second_sums, first_sums, rim_part, second_prev, first_prev, inner_rim, stage, in_vmem(time_held)),
        out_specs=HBM,
    )


def solution(mesh):
    placed = (P("tm", "rows", None, None), P(), P(), P(), P())
    return jax.shard_map(
        shards, mesh=mesh, in_specs=placed, out_specs=P("tm", "rows", None, None), check_vma=False
    )
```
